512 devices in a mesh: context: 64 (over z_hi, y, core), tensor: 8 (over z_lo, x).
Axes of the slice: x: 4, y: 8, z: 8 (z_hi: 4, z_lo: 2; z = z_hi * 2 + z_lo), core: 2. Of those that a mesh axis runs over, the one named last changes fastest.
Arguments:
- query_slab: bfloat16 [4096, 8192], P('tensor', 'context'), may hold values from -6 to 6
- key_slab: bfloat16 [4096, 8192], P('tensor', 'context'), may hold values from -6 to 6
- value_slab: bfloat16 [4096, 8192], P('tensor', 'context'), may hold values from -6 to 6
- cotangent: bfloat16 [4096, 8192], P('tensor', 'context'), may hold values from -6 to 6
- filters: bfloat16 [256, 8192], P('tensor', 'context'), may hold values from -2 to 2
- skip_gain: float32 [4096], P('tensor'), may hold values from -1 to 1
Outputs:
- mixed: bfloat16 [4096, 8192], P('tensor', 'context')
- grad_query: bfloat16 [4096, 8192], P('tensor', 'context')
- grad_key: bfloat16 [4096, 8192], P('tensor', 'context')
- grad_value: bfloat16 [4096, 8192], P('tensor', 'context')
- filter_grad: float32 [256, 8192], P('tensor', 'context')
The draws below stay inside these ranges and needn't reach their ends.
All inputs are finite; a program needn't handle non-finite values.
Results may differ from the reference program's by a relative error of at most 0.0095.
Values may be sent and summed in bfloat16 or wider, within the bound.
A program may use at most 64 MiB of HBM per device.

```python
import math
import jax
import jax.numpy as jnp
from jax import lax

LENGTH = 8192
CHANNELS = 4096
GROUP = 16
GROUPS = 256


def draw_filters(key, part):
    key = jax.random.fold_in(key, 7)
    span_key, tap_key = jax.random.split(key)
    tap_index = jnp.arange(LENGTH, dtype=jnp.float32)[None, :]
    decay_len = jnp.exp(jax.random.uniform(span_key, (GROUPS, 1), jnp.float32, math.log(32.0), math.log(4.0 * LENGTH)))
    rough_part = jax.random.normal(tap_key, (GROUPS, LENGTH), jnp.float32)
    envelope = jnp.exp(-tap_index / decay_len) * jax.lax.rsqrt(jnp.minimum(decay_len, 1.0 * LENGTH))
    return (rough_part * envelope).astype(jnp.bfloat16)


def level_of(stream_key, shape, pieces, least, top_value):
    gain = 1.0
    for position, blocks in pieces:
        steps = jax.random.uniform(jax.random.fold_in(jax.random.fold_in(stream_key, 6), position), (blocks,), jnp.float32, least / len(pieces), top_value / len(pieces))
        gain = gain * jnp.repeat(jnp.exp(steps), shape[position] // blocks).reshape((-1,) + (1,) * (len(shape) - 1 - position))
    return gain


def noise(own_key, dims, width, reach, cuts=(), kind=jnp.bfloat16):
    values = width * jax.random.normal(own_key, dims, jnp.float32)
    if cuts:
        values = values * level_of(own_key, dims, cuts, -0.22, 0.18)
    return jnp.clip(values, -reach, reach).astype(kind)


def setup_inputs(seed: int = 0) -> dict:
    arg_keys = jax.random.split(jax.random.key(seed), 7)
    return {
        "query_slab": noise(arg_keys[0], (CHANNELS, LENGTH), 1.0, 6.0, ((0, 8), (1, 64))),
        "key_slab": noise(arg_keys[1], (CHANNELS, LENGTH), 1.0, 6.0, ((0, 8), (1, 64))),
        "value_slab": noise(arg_keys[2], (CHANNELS, LENGTH), 1.0, 6.0, ((0, 8), (1, 64))),
        "cotangent": noise(arg_keys[3], (CHANNELS, LENGTH), 1.0, 6.0, ((0, 8), (1, 64))),
        "filters": draw_filters(jax.random.fold_in(arg_keys[6], 71), 0),
        "skip_gain": jnp.clip(jax.random.uniform(arg_keys[5], (CHANNELS,), jnp.float32, -1.0, 1.0) * level_of(arg_keys[5], (CHANNELS,), ((0, 8),), -0.4, 0.0), -1.0, 1.0),
    }


def group_terms(items):
    own_product, own_grad, own_filter = items
    padded = 2 * LENGTH
    spec_prod = jnp.fft.rfft(own_product.astype(jnp.float32), n=padded, axis=-1)
    spec_grad = jnp.fft.rfft(own_grad.astype(jnp.float32), n=padded, axis=-1)
    spec_filter = jnp.fft.rfft(own_filter.astype(jnp.float32), n=padded, axis=-1)
    conv_part = jnp.fft.irfft(spec_prod * spec_filter[None, :], n=padded, axis=-1)[:, :LENGTH]
    corr_part = jnp.fft.irfft(spec_grad * jnp.conj(spec_filter)[None, :], n=padded, axis=-1)[:, :LENGTH]
    cross_sum = lax.optimization_barrier(jnp.sum(spec_grad * jnp.conj(spec_prod), axis=0))
    grad_part = jnp.fft.irfft(cross_sum, n=padded, axis=-1)[:LENGTH]
    return (conv_part.astype(jnp.bfloat16), corr_part.astype(jnp.bfloat16), grad_part.astype(jnp.float32))

def reference(query_slab, key_slab, value_slab, cotangent, filters, skip_gain):
    product = (key_slab.astype(jnp.float32) * value_slab.astype(jnp.float32)).astype(jnp.bfloat16)
    grad_mix = (cotangent.astype(jnp.float32) * query_slab.astype(jnp.float32)).astype(jnp.bfloat16)
    conv_all, corr_all, raw_grad = lax.map(group_terms, (product.reshape(GROUPS, GROUP, LENGTH), grad_mix.reshape(GROUPS, GROUP, LENGTH), filters))
    conv_all = conv_all.reshape(CHANNELS, LENGTH).astype(jnp.float32)
    corr_all = corr_all.reshape(CHANNELS, LENGTH).astype(jnp.float32)
    gain_col = skip_gain[:, None]
    forward_sum = conv_all + gain_col * product.astype(jnp.float32)
    mixed = (query_slab.astype(jnp.float32) * forward_sum).astype(jnp.bfloat16)
    grad_query = (cotangent.astype(jnp.float32) * forward_sum).astype(jnp.bfloat16)
    back_sum = corr_all + gain_col * grad_mix.astype(jnp.float32)
    grad_key = (back_sum * value_slab.astype(jnp.float32)).astype(jnp.bfloat16)
    grad_value = (back_sum * key_slab.astype(jnp.float32)).astype(jnp.bfloat16)
    grad_size = jnp.sqrt(jnp.sum(raw_grad * raw_grad) + 1e-06)
    factor = jnp.minimum(1.0, math.sqrt(GROUPS * LENGTH) / grad_size)
    filter_grad = (raw_grad * factor).astype(jnp.float32)
    return (mixed, grad_query, grad_key, grad_value, filter_grad)
```

```python
import functools
import math

import jax
import jax.numpy as jnp
from jax import lax
from jax.experimental import pallas as pl
from jax.experimental.pallas import tpu as pltpu
from jax.sharding import PartitionSpec as P

MESH = pl.DeviceIdType.MESH
F32 = jnp.float32
BF16 = jnp.bfloat16
LANES = 128
OWN = 8


def exchange(lanes=LANES):
    row = lax.broadcasted_iota(jnp.int32, (lanes, lanes), 0)
    col = lax.broadcasted_iota(jnp.int32, (lanes, lanes), 1)
    return (row + col == lanes - 1).astype(BF16)


def kernel(
    C, T, entries,
    q_hbm, k_hbm, v_hbm, c_hbm, f_hbm, gain_hbm,
    mixed_ref, gq_ref, gk_ref, gv_ref, fg_ref,
    q_ref, k_ref, v_ref, c_ref, f_ref, gain_ref,
    gain_col, fsend, frecv, msend, mrecv, toep, z2, acc, gcat, bsend, brecv,
    raw, raw_other, gsend, grecv, tsend, trecv,
    load_sem, send_sem, recv_sem,
):
    me = lax.axis_index("context")
    ten = lax.axis_index("tensor")
    half = C // 2
    pair = me // 2
    core = me % 2
    rows = C * OWN

    loads = [
        pltpu.make_async_copy(src, dst, load_sem.at[n])
        for n, (src, dst) in enumerate(
            [(f_hbm, f_ref), (k_hbm, k_ref), (v_hbm, v_ref), (q_hbm, q_ref), (c_hbm, c_ref), (gain_hbm, gain_ref)]
        )
    ]
    for load in loads:
        load.start()

    def context_peer(k):
        return lax.rem(me + k, C)

    barrier = pltpu.get_barrier_semaphore()

    def greet(k, _):
        pl.semaphore_signal(barrier, inc=1, device_id=(context_peer(k), ten), device_id_type=MESH)
        return 0

    lax.fori_loop(1, C, greet, 0)
    for k in range(1, T):
        pl.semaphore_signal(barrier, inc=1, device_id=(me, lax.rem(ten + k, T)), device_id_type=MESH)

    flip = exchange()

    loads[0].wait()
    taps = jnp.dot(f_ref[...], flip, preferred_element_type=F32)
    for r in range(half):
        fsend[r] = taps[r : r + 1]

    for load in loads[1:5]:
        load.wait()
    product = (k_ref[...].astype(F32) * v_ref[...].astype(F32)).astype(BF16)
    mirrored = jnp.dot(product, flip, preferred_element_type=F32).reshape(C, OWN, LANES)
    gmix = (q_ref[...].astype(F32) * c_ref[...].astype(F32)).reshape(C, OWN, LANES)
    msend[...] = jnp.concatenate([mirrored, gmix], axis=1).astype(BF16)

    pl.semaphore_wait(barrier, C - 1 + T - 1)

    def send(src, dst, phase, peer):
        return pltpu.make_async_remote_copy(
            src_ref=src, dst_ref=dst, send_sem=send_sem.at[phase], recv_sem=recv_sem.at[phase],
            device_id=peer, device_id_type=MESH,
        )

    def send_taps(k, _):
        to = context_peer(k)
        send(fsend.at[to // 2], frecv.at[me], 0, (to, ten)).start()
        return 0

    def send_main(k, _):
        to = context_peer(k)
        send(msend.at[to], mrecv.at[me], 1, (to, ten)).start()
        return 0

    lax.fori_loop(1, C, send_taps, 0)
    lax.fori_loop(1, C, send_main, 0)

    frecv[me] = fsend[pair]
    mrecv[me] = msend[me]
    loads[5].wait()
    for n in range(gain_ref.shape[0]):
        wide = jnp.broadcast_to(gain_ref[n : n + 1, :], (LANES, LANES))
        gain_col[n * LANES : (n + 1) * LANES, :] = wide.T
    toep[0] = jnp.zeros((LANES, LANES), BF16)
    z2[half * 16 :, :] = jnp.zeros((z2.shape[0] - half * 16, 2 * LANES), BF16)
    gcat[rows:, :] = jnp.zeros((gcat.shape[0] - rows, 2 * LANES), BF16)

    send(frecv.at[pl.ds(0, C - 1)], frecv.at[pl.ds(0, C - 1)], 0, (me, ten)).wait_recv()
    row = lax.broadcasted_iota(jnp.int32, (LANES, LANES), 0)
    col = lax.broadcasted_iota(jnp.int32, (LANES, LANES), 1)
    lower = col <= row

    def build(d, last):
        wide = jnp.broadcast_to(frecv[d], (LANES, LANES))
        turned = pltpu.roll(wide, 1, 1, stride=1, stride_axis=0)
        toep[d + 1] = jnp.where(lower, turned, last).astype(BF16)
        return turned

    lax.fori_loop(0, C, build, jnp.zeros((LANES, LANES), F32))

    send(mrecv.at[pl.ds(0, C - 1)], mrecv.at[pl.ds(0, C - 1)], 1, (me, ten)).wait_recv()
    zero = jnp.zeros((OWN, LANES), F32)
    for j in range(half):
        two = []
        for i in (2 * j, 2 * j + 1):
            two.append(jnp.concatenate([mrecv[C - 1 - i].astype(F32)[:OWN], mrecv[i].astype(F32)[OWN:]], axis=0))
        z2[16 * j : 16 * j + 16, :] = jnp.concatenate(two, axis=1).astype(BF16)

    def weight(d):
        top = jnp.concatenate([toep[2 * d + 1], toep[2 * d]], axis=1)
        low = jnp.concatenate([toep[2 * d + 2], toep[2 * d + 1]], axis=1)
        return jnp.concatenate([top, low], axis=0)

    step = min(4, half)
    for d0 in range(0, half, step):
        size = 16 * (half - d0)
        left = jnp.concatenate([z2[16 * (d0 + u) : 16 * (d0 + u) + size, :] for u in range(step)], axis=1)
        right = jnp.concatenate([weight(d0 + u) for u in range(step)], axis=0)
        part = jnp.dot(left, right, preferred_element_type=F32)
        if d0 == 0:
            acc[...] = part
        else:
            acc[0:size, :] += part

    for i in range(C):
        m = C - 1 - i
        conv = acc[16 * (m // 2) : 16 * (m // 2) + OWN, (m % 2) * LANES : (m % 2 + 1) * LANES]
        corr = acc[16 * (i // 2) + OWN : 16 * (i // 2) + 16, (i % 2) * LANES : (i % 2 + 1) * LANES]
        bsend[i] = jnp.concatenate([conv, corr], axis=0).astype(BF16)

    def send_back(k, _):
        to = context_peer(k)
        send(bsend.at[to], brecv.at[me], 2, (to, ten)).start()
        return 0

    lax.fori_loop(1, C, send_back, 0)
    brecv[me] = bsend[me]

    whole = mrecv[...].astype(F32)
    xt = whole[:, :OWN].reshape(rows, LANES).T.astype(BF16)
    gpart = whole[:, OWN:]
    after = jnp.concatenate([gpart[1:], zero[None]], axis=0)
    gcat[0:rows, :] = jnp.concatenate([gpart, after], axis=2).reshape(rows, 2 * LANES).astype(BF16)

    def lags(e, depth):
        first = pl.multiple_of(16 * e, 16)
        return jnp.dot(xt[:, :depth], gcat[pl.ds(first, depth), :], preferred_element_type=F32)

    def skew(block):
        return pltpu.roll(block, 1, 1, stride=1, stride_axis=0)

    def gather(depth, group):
        def body(n, last):
            parts = [lags(group * n + u, depth) for u in range(group)]
            for u in reversed(range(group)):
                for side in (1, 0):
                    turned = skew(parts[u][:, side * LANES : (side + 1) * LANES])
                    place = 2 * (group * n + u) + side
                    raw[place] = jnp.sum(jnp.where(lower, turned, last), axis=0, keepdims=True)
                    last = turned
            return last

        return body

    group = min(4, half // 2)
    quarter = half // 2 // group
    last = jnp.zeros((LANES, LANES), F32)
    late = gather(rows // 2, group)
    early = gather(rows, group)
    last = lax.fori_loop(0, quarter, lambda n, s: late(2 * quarter - 1 - n, s), last)
    last = lax.fori_loop(0, quarter, lambda n, s: early(quarter - 1 - n, s), last)

    other = me + 1 - 2 * core
    swap = send(raw, raw_other, 3, (other, ten))
    swap.start()
    swap.wait_recv()
    total = raw[...] + raw_other[...]
    size2 = jnp.sum(jnp.sum(total * total, axis=0), axis=1, keepdims=True)
    size_row = jnp.broadcast_to(size2, (1, LANES))
    for i in range(C):
        gsend[i] = jnp.concatenate([total[i], size_row], axis=0)

    base = half * core
    offset = lax.rem(me, half)
    mine = core == me // half

    def send_grad(k, _):
        to = base + lax.rem(offset + k, half)
        send(gsend.at[to], grecv.at[pair], 4, (to, ten)).start()
        return 0

    lax.fori_loop(1, half, send_grad, 0)
    straight = base + offset

    @pl.when(mine)
    def _():
        grecv[pair] = gsend[me]

    @pl.when(jnp.logical_not(mine))
    def _():
        send(gsend.at[straight], grecv.at[pair], 4, (straight, ten)).start()

    def grads(count):
        part = pl.ds(0, count)
        return send(gsend.at[part], grecv.at[part], 4, (me, ten))

    @pl.when(mine)
    def _():
        grads(half - 1).wait_recv()

    @pl.when(jnp.logical_not(mine))
    def _():
        grads(half).wait_recv()

    square = jnp.sum(grecv[:, 1:2, :], axis=0)
    tsend[...] = square
    trecv[ten] = square
    for k in range(1, T):
        send(tsend, trecv.at[ten], 5, (me, lax.rem(ten + k, T))).start()

    send(brecv.at[pl.ds(0, C - 1)], brecv.at[pl.ds(0, C - 1)], 2, (me, ten)).wait_recv()
    back = brecv[...].astype(F32)
    conv = jnp.dot(back[:, :OWN].reshape(rows, LANES).astype(BF16), flip, preferred_element_type=F32)
    corr = back[:, OWN:].reshape(rows, LANES)
    gain = gain_col[...]
    kf = k_ref[...].astype(F32)
    vf = v_ref[...].astype(F32)
    forward = conv + gain * (kf * vf).astype(BF16).astype(F32)
    qf = q_ref[...].astype(F32)
    cf = c_ref[...].astype(F32)
    mixed_ref[...] = (qf * forward).astype(BF16)
    gq_ref[...] = (cf * forward).astype(BF16)
    backward = corr + gain * (qf * cf).astype(BF16).astype(F32)
    gk_ref[...] = (backward * vf).astype(BF16)
    gv_ref[...] = (backward * kf).astype(BF16)

    if T > 1:
        part = pl.ds(0, T - 1)
        send(trecv.at[part], trecv.at[part], 5, (me, ten)).wait_recv()
    squared = jnp.sum(trecv[...], axis=0)
    factor = jnp.minimum(1.0, math.sqrt(entries) / jnp.sqrt(squared + 1e-6))
    for r in range(half):
        fg_ref[r : r + 1, :] = grecv[r, 0:1, :] * factor

    send(frecv.at[pl.ds(0, C - 1)], frecv.at[pl.ds(0, C - 1)], 0, (me, ten)).wait_send()
    send(msend.at[pl.ds(0, C - 1)], msend.at[pl.ds(0, C - 1)], 1, (me, ten)).wait_send()
    send(bsend.at[pl.ds(0, C - 1)], bsend.at[pl.ds(0, C - 1)], 2, (me, ten)).wait_send()
    swap.wait_send()

    @pl.when(mine)
    def _():
        grads(half - 1).wait_send()

    @pl.when(jnp.logical_not(mine))
    def _():
        grads(half).wait_send()

    if T > 1:
        part = pl.ds(0, T - 1)
        send(trecv.at[part], trecv.at[part], 5, (me, ten)).wait_send()


def per_device(C, T, query_slab, key_slab, value_slab, cotangent, filters, skip_gain):
    channels, tokens = query_slab.shape
    half = C // 2
    rows = C * OWN
    entries = half * T * tokens * C
    slab = jax.ShapeDtypeStruct((channels, tokens), BF16)
    gains = skip_gain.reshape(channels // LANES, LANES)
    any_spec = pl.BlockSpec(memory_space=pl.ANY)
    vmem_spec = pl.BlockSpec(memory_space=pltpu.VMEM)
    return pl.pallas_call(
        functools.partial(kernel, C, T, entries),
        out_shape=(slab, slab, slab, slab, jax.ShapeDtypeStruct((half, tokens), F32)),
        in_specs=[any_spec] * 6,
        out_specs=(vmem_spec,) * 5,
        scratch_shapes=[
            pltpu.VMEM((channels, tokens), BF16),
            pltpu.VMEM((channels, tokens), BF16),
            pltpu.VMEM((channels, tokens), BF16),
            pltpu.VMEM((channels, tokens), BF16),
            pltpu.VMEM((half, tokens), BF16),
            pltpu.VMEM(gains.shape, F32),
            pltpu.VMEM((channels, LANES), F32),
            pltpu.VMEM((half, 1, LANES), F32),
            pltpu.VMEM((C, 1, LANES), F32),
            pltpu.VMEM((C, 16, LANES), BF16),
            pltpu.VMEM((C, 16, LANES), BF16),
            pltpu.VMEM((C + 1, LANES, LANES), BF16),
            pltpu.VMEM((16 * (half + 4), 2 * LANES), BF16),
            pltpu.VMEM((16 * half, 2 * LANES), F32),
            pltpu.VMEM((2 * rows, 2 * LANES), BF16),
            pltpu.VMEM((C, 16, LANES), BF16),
            pltpu.VMEM((C, 16, LANES), BF16),
            pltpu.VMEM((C, 1, LANES), F32),
            pltpu.VMEM((C, 1, LANES), F32),
            pltpu.VMEM((C, 2, LANES), F32),
            pltpu.VMEM((half, 2, LANES), F32),
            pltpu.VMEM((1, LANES), F32),
            pltpu.VMEM((T, 1, LANES), F32),
            pltpu.SemaphoreType.DMA((6,)),
            pltpu.SemaphoreType.DMA((6,)),
            pltpu.SemaphoreType.DMA((6,)),
        ],
        compiler_params=pltpu.CompilerParams(
            collective_id=0, has_side_effects=True, vmem_limit_bytes=40 * 1024 * 1024
        ),
        name="hyena",
    )(query_slab, key_slab, value_slab, cotangent, filters, gains)


def solution(mesh):
    C, T = mesh.shape["context"], mesh.shape["tensor"]
    slab = P("tensor", "context")
    return jax.shard_map(
        functools.partial(per_device, C, T),
        mesh=mesh,
        in_specs=(slab, slab, slab, slab, slab, P("tensor")),
        out_specs=(slab, slab, slab, slab, slab),
        check_vma=False,
    )
```

```python
import functools
import math

import jax
import jax.numpy as jnp
from jax import lax
from jax.experimental import pallas as pl
from jax.experimental.pallas import tpu as pltpu
from jax.sharding import PartitionSpec as P

MESH = pl.DeviceIdType.MESH
F32 = jnp.float32
BF16 = jnp.bfloat16
LANES = 128
VMEM_BYTES = 62 * 1024 * 1024
UNROLL = 8
OWN = 8


def exchange(lanes=LANES):
    row = lax.broadcasted_iota(jnp.int32, (lanes, lanes), 0)
    col = lax.broadcasted_iota(jnp.int32, (lanes, lanes), 1)
    return (row + col == lanes - 1).astype(BF16)


def far(i, n):
    return n // 2 + ((i + 1) // 2) * (1 - 2 * (i % 2))


def kernel(
    C, T,
    q_hbm, k_hbm, v_hbm, c_hbm, f_hbm,
    brecv, grads_out, trecv,
    q_ref, k_ref, v_ref, c_ref, f_ref,
    fsend, frecv, msend, mrecv, toep, z2, acc, gcat, bsend,
    raw, raw_other, gsend, grecv, tsend,
    load_sem, send_sem, recv_sem,
):
    me = lax.axis_index("context")
    ten = lax.axis_index("tensor")
    half = C // 2
    Z = max(1, C // 16)
    Y = half // Z
    pair = me // 2
    core = me % 2
    rows = C * OWN

    loads = [
        pltpu.make_async_copy(src, dst, load_sem.at[n])
        for n, (src, dst) in enumerate(
            [(f_hbm, f_ref), (k_hbm, k_ref), (v_hbm, v_ref), (q_hbm, q_ref), (c_hbm, c_ref)]
        )
    ]
    for load in loads:
        load.start()

    def each_peer(start, cores=2):
        y = pair % Y
        columns = []
        for j in range(Z):
            z = lax.rem(pair // Y + far(j, Z), Z)
            columns += [2 * Y * z + 1 - core, 2 * Y * z + core][2 - cores :]

        def ring(i, _):
            place = 2 * lax.rem(y + far(i, Y), Y)
            for column in columns:
                start(column + place)
            return 0

        lax.fori_loop(0, Y - 1, ring, 0)
        for column in columns[:-1]:
            start(column + 2 * y)

    barrier = pltpu.get_barrier_semaphore()
    each_peer(lambda to: pl.semaphore_signal(barrier, inc=1, device_id=(to, ten), device_id_type=MESH))
    for k in range(1, T):
        pl.semaphore_signal(barrier, inc=1, device_id=(me, lax.rem(ten + k, T)), device_id_type=MESH)

    flip = exchange()

    loads[0].wait()
    taps = jnp.dot(f_ref[...], flip, preferred_element_type=F32)
    for r in range(half):
        fsend[r] = taps[r : r + 1]

    for load in loads[1:5]:
        load.wait()
    product = (k_ref[...].astype(F32) * v_ref[...].astype(F32)).astype(BF16)
    mirrored = jnp.dot(product, flip, preferred_element_type=F32).reshape(C, OWN, LANES)
    gmix = (q_ref[...].astype(F32) * c_ref[...].astype(F32)).reshape(C, OWN, LANES)
    msend[...] = jnp.concatenate([mirrored, gmix], axis=1).astype(BF16)

    pl.semaphore_wait(barrier, C - 1 + T - 1)

    def send(src, dst, phase, peer):
        return pltpu.make_async_remote_copy(
            src_ref=src, dst_ref=dst, send_sem=send_sem.at[phase], recv_sem=recv_sem.at[phase],
            device_id=peer, device_id_type=MESH,
        )

    each_peer(lambda to: send(msend.at[to], mrecv.at[me], 1, (to, ten)).start())
    each_peer(lambda to: send(fsend.at[to // 2], frecv.at[core, pair], 0, (to, ten)).start(), cores=1)

    frecv[core, pair] = fsend[pair]
    mrecv[me] = msend[me]
    toep[0] = jnp.zeros((LANES, LANES), BF16)
    z2[half * 16 :, :] = jnp.zeros((z2.shape[0] - half * 16, 2 * LANES), BF16)
    gcat[rows:, :] = jnp.zeros((gcat.shape[0] - rows, 2 * LANES), BF16)

    row = lax.broadcasted_iota(jnp.int32, (LANES, LANES), 0)
    col = lax.broadcasted_iota(jnp.int32, (LANES, LANES), 1)
    lower = col <= row

    send(mrecv.at[pl.ds(0, C - 1)], mrecv.at[pl.ds(0, C - 1)], 1, (me, ten)).wait_recv()
    zero = jnp.zeros((OWN, LANES), F32)
    other = me + 1 - 2 * core
    some_taps = frecv.at[core, pl.ds(0, half - 1)]
    send(some_taps, some_taps, 0, (me, ten)).wait_recv()
    tap_swap = send(frecv.at[core], frecv.at[core], 6, (other, ten))
    tap_swap.start()

    whole = mrecv[...].astype(F32)
    xt = whole[:, :OWN].reshape(rows, LANES).T.astype(BF16)
    gpart = whole[:, OWN:]
    after = jnp.concatenate([gpart[1:], zero[None]], axis=0)
    gcat[0:rows, :] = jnp.concatenate([gpart, after], axis=2).reshape(rows, 2 * LANES).astype(BF16)

    def lags(e, depth):
        first = pl.multiple_of(16 * e, 16)
        return jnp.dot(xt[:, :depth], gcat[pl.ds(first, depth), :], preferred_element_type=F32)

    def skew(block):
        return pltpu.roll(block, 1, 1, stride=1, stride_axis=0)

    def gather(depth, group):
        def body(n, last):
            parts = [lags(group * n + u, depth) for u in range(group)]
            for u in reversed(range(group)):
                for side in (1, 0):
                    turned = skew(parts[u][:, side * LANES : (side + 1) * LANES])
                    place = 2 * (group * n + u) + side
                    raw[place] = jnp.sum(jnp.where(lower, turned, last), axis=0, keepdims=True)
                    last = turned
            return last

        return body

    group = min(4, half // 2)
    quarter = half // 2 // group
    last = jnp.zeros((LANES, LANES), F32)
    late = gather(rows // 2, group)
    early = gather(rows, group)
    last = lax.fori_loop(0, quarter, lambda n, s: late(2 * quarter - 1 - n, s), last)
    last = lax.fori_loop(0, quarter, lambda n, s: early(quarter - 1 - n, s), last)

    swap = send(raw, raw_other, 3, (other, ten))
    swap.start()

    tap_swap.wait_recv()
    def build(n, last):
        for u in range(UNROLL):
            d = UNROLL * n + u
            turned = skew(jnp.broadcast_to(frecv[u % 2, d // 2], (LANES, LANES)))
            toep[d + 1] = jnp.where(lower, turned, last).astype(BF16)
            last = turned
        return last

    lax.fori_loop(0, C // UNROLL, build, jnp.zeros((LANES, LANES), F32))

    for j in range(half):
        two = []
        for i in (2 * j, 2 * j + 1):
            two.append(jnp.concatenate([mrecv[C - 1 - i].astype(F32)[:OWN], mrecv[i].astype(F32)[OWN:]], axis=0))
        z2[16 * j : 16 * j + 16, :] = jnp.concatenate(two, axis=1).astype(BF16)

    swap.wait_recv()
    total = raw[...] + raw_other[...]
    size2 = jnp.sum(jnp.sum(total * total, axis=0), axis=1, keepdims=True)
    size_row = jnp.broadcast_to(size2, (1, LANES))
    for i in range(C):
        gsend[i] = jnp.concatenate([total[i], size_row], axis=0)

    base = half * core
    offset = lax.rem(me, half)
    mine = core == me // half

    def send_grad(k, _):
        to = base + lax.rem(offset + k, half)
        send(gsend.at[to], grecv.at[pair], 4, (to, ten)).start()
        return 0

    lax.fori_loop(1, half, send_grad, 0)
    straight = base + offset

    @pl.when(mine)
    def _():
        grecv[pair] = gsend[me]

    @pl.when(jnp.logical_not(mine))
    def _():
        send(gsend.at[straight], grecv.at[pair], 4, (straight, ten)).start()

    def weight(d):
        top = jnp.concatenate([toep[2 * d + 1], toep[2 * d]], axis=1)
        low = jnp.concatenate([toep[2 * d + 2], toep[2 * d + 1]], axis=1)
        return jnp.concatenate([top, low], axis=0)

    step = min(4, half)
    for d0 in range(0, half, step):
        size = 16 * (half - d0)
        left = jnp.concatenate([z2[16 * (d0 + u) : 16 * (d0 + u) + size, :] for u in range(step)], axis=1)
        right = jnp.concatenate([weight(d0 + u) for u in range(step)], axis=0)
        part = jnp.dot(left, right, preferred_element_type=F32)
        if d0 == 0:
            acc[...] = part
        else:
            acc[0:size, :] += part

    for i in range(C):
        m = C - 1 - i
        conv = acc[16 * (m // 2) : 16 * (m // 2) + OWN, (m % 2) * LANES : (m % 2 + 1) * LANES]
        corr = acc[16 * (i // 2) + OWN : 16 * (i // 2) + 16, (i % 2) * LANES : (i % 2 + 1) * LANES]
        bsend[i] = jnp.concatenate([conv, corr], axis=0).astype(BF16)

    each_peer(lambda to: send(bsend.at[to], brecv.at[me], 2, (to, ten)).start())
    own_back = pltpu.make_async_copy(bsend.at[me], brecv.at[me], load_sem.at[0])
    own_back.start()

    def grads(count):
        part = pl.ds(0, count)
        return send(gsend.at[part], grecv.at[part], 4, (me, ten))

    @pl.when(mine)
    def _():
        grads(half - 1).wait_recv()

    @pl.when(jnp.logical_not(mine))
    def _():
        grads(half).wait_recv()

    square = jnp.sum(grecv[:, 1:2, :], axis=0)
    tsend[...] = square
    own_size = pltpu.make_async_copy(tsend, trecv.at[ten], load_sem.at[1])
    own_size.start()
    own_grads = pltpu.make_async_copy(grecv, grads_out, load_sem.at[2])
    own_grads.start()
    for k in range(1, T):
        send(tsend, trecv.at[ten], 5, (me, lax.rem(ten + k, T))).start()

    send(brecv.at[pl.ds(0, C - 1)], brecv.at[pl.ds(0, C - 1)], 2, (me, ten)).wait_recv()
    if T > 1:
        part = pl.ds(0, T - 1)
        send(trecv.at[part], trecv.at[part], 5, (me, ten)).wait_recv()
    own_back.wait()
    own_grads.wait()
    own_size.wait()

    send(some_taps, some_taps, 0, (me, ten)).wait_send()
    tap_swap.wait_send()
    send(msend.at[pl.ds(0, C - 1)], msend.at[pl.ds(0, C - 1)], 1, (me, ten)).wait_send()
    send(bsend.at[pl.ds(0, C - 1)], bsend.at[pl.ds(0, C - 1)], 2, (me, ten)).wait_send()
    swap.wait_send()

    @pl.when(mine)
    def _():
        grads(half - 1).wait_send()

    @pl.when(jnp.logical_not(mine))
    def _():
        grads(half).wait_send()

    if T > 1:
        part = pl.ds(0, T - 1)
        send(trecv.at[part], trecv.at[part], 5, (me, ten)).wait_send()


def gates(
    C, T, entries,
    q_hbm, k_hbm, v_hbm, c_hbm, gain_hbm, back_hbm, grads_hbm, sizes_hbm,
    mixed_hbm, gq_hbm, gk_hbm, gv_hbm, fg_hbm,
    q_ref, k_ref, v_ref, c_ref, gain_ref, back, grads, sizes,
    mixed, gq, gk, gv, fg, gain_col, load_sem, store_sem,
):
    half = C // 2
    rows = C * OWN
    pairs = [
        (q_hbm, q_ref), (k_hbm, k_ref), (v_hbm, v_ref), (c_hbm, c_ref), (back_hbm, back),
        (gain_hbm, gain_ref), (grads_hbm, grads), (sizes_hbm, sizes),
    ]
    loads = [pltpu.make_async_copy(src, dst, load_sem.at[n]) for n, (src, dst) in enumerate(pairs)]
    for load in loads:
        load.start()
    outs = [(mixed, mixed_hbm), (gq, gq_hbm), (gk, gk_hbm), (gv, gv_hbm), (fg, fg_hbm)]
    stores = [pltpu.make_async_copy(src, dst, store_sem.at[n]) for n, (src, dst) in enumerate(outs)]
    flip = exchange()
    for load in loads:
        load.wait()

    for n in range(rows // LANES):
        wide = jnp.broadcast_to(gain_ref[n : n + 1, :], (LANES, LANES))
        gain_col[n * LANES : (n + 1) * LANES, :] = wide.T
    gain = gain_col[...]
    both = back[...].astype(F32)
    conv = jnp.dot(both[:, :OWN].reshape(rows, LANES).astype(BF16), flip, preferred_element_type=F32)
    corr = both[:, OWN:].reshape(rows, LANES)
    kf = k_ref[...].astype(F32)
    vf = v_ref[...].astype(F32)
    qf = q_ref[...].astype(F32)
    cf = c_ref[...].astype(F32)
    backward = corr + gain * (qf * cf).astype(BF16).astype(F32)
    gk[...] = (backward * vf).astype(BF16)
    stores[2].start()
    gv[...] = (backward * kf).astype(BF16)
    stores[3].start()
    forward = conv + gain * (kf * vf).astype(BF16).astype(F32)
    mixed[...] = (qf * forward).astype(BF16)
    stores[0].start()
    gq[...] = (cf * forward).astype(BF16)
    stores[1].start()

    squared = jnp.sum(sizes[...], axis=0)
    factor = jnp.minimum(1.0, math.sqrt(entries) / jnp.sqrt(squared + 1e-6))
    for r in range(half):
        fg[r : r + 1, :] = grads[r, 0:1, :] * factor
    stores[4].start()
    for store in stores:
        store.wait()


def per_device(C, T, query_slab, key_slab, value_slab, cotangent, filters, skip_gain):
    channels, tokens = query_slab.shape
    half = C // 2
    rows = C * OWN
    entries = half * T * tokens * C
    gains = skip_gain.reshape(channels // LANES, LANES)
    hbm_spec = pl.BlockSpec(memory_space=pltpu.HBM)
    back = jax.ShapeDtypeStruct((C, 16, LANES), BF16)
    grads = jax.ShapeDtypeStruct((half, 2, LANES), F32)
    sizes = jax.ShapeDtypeStruct((T, 1, LANES), F32)
    came = pl.pallas_call(
        functools.partial(kernel, C, T),
        out_shape=(back, grads, sizes),
        in_specs=[hbm_spec] * 5,
        out_specs=(hbm_spec,) * 3,
        scratch_shapes=[
            pltpu.VMEM((channels, tokens), BF16),
            pltpu.VMEM((channels, tokens), BF16),
            pltpu.VMEM((channels, tokens), BF16),
            pltpu.VMEM((channels, tokens), BF16),
            pltpu.VMEM((half, tokens), BF16),
            pltpu.VMEM((half, 1, LANES), F32),
            pltpu.VMEM((2, half, 1, LANES), F32),
            pltpu.VMEM((C, 16, LANES), BF16),
            pltpu.VMEM((C, 16, LANES), BF16),
            pltpu.VMEM((C + 1, LANES, LANES), BF16),
            pltpu.VMEM((16 * (half + 4), 2 * LANES), BF16),
            pltpu.VMEM((16 * half, 2 * LANES), F32),
            pltpu.VMEM((2 * rows, 2 * LANES), BF16),
            pltpu.VMEM((C, 16, LANES), BF16),
            pltpu.VMEM((C, 1, LANES), F32),
            pltpu.VMEM((C, 1, LANES), F32),
            pltpu.VMEM((C, 2, LANES), F32),
            pltpu.VMEM((half, 2, LANES), F32),
            pltpu.VMEM((1, LANES), F32),
            pltpu.SemaphoreType.DMA((7,)),
            pltpu.SemaphoreType.DMA((7,)),
            pltpu.SemaphoreType.DMA((7,)),
        ],
        compiler_params=pltpu.CompilerParams(
            collective_id=0, has_side_effects=True, vmem_limit_bytes=VMEM_BYTES
        ),
        name="hyena",
    )(query_slab, key_slab, value_slab, cotangent, filters)
    slab = jax.ShapeDtypeStruct((channels, tokens), BF16)
    slab_buffer = pltpu.VMEM((channels, tokens), BF16)
    return pl.pallas_call(
        functools.partial(gates, C, T, entries),
        out_shape=(slab, slab, slab, slab, jax.ShapeDtypeStruct((half, tokens), F32)),
        in_specs=[hbm_spec] * 8,
        out_specs=(hbm_spec,) * 5,
        scratch_shapes=[
            slab_buffer, slab_buffer, slab_buffer, slab_buffer,
            pltpu.VMEM(gains.shape, F32),
            pltpu.VMEM(back.shape, BF16),
            pltpu.VMEM(grads.shape, F32),
            pltpu.VMEM(sizes.shape, F32),
            slab_buffer, slab_buffer, slab_buffer, slab_buffer,
            pltpu.VMEM((half, tokens), F32),
            pltpu.VMEM((channels, LANES), F32),
            pltpu.SemaphoreType.DMA((8,)),
            pltpu.SemaphoreType.DMA((5,)),
        ],
        compiler_params=pltpu.CompilerParams(vmem_limit_bytes=VMEM_BYTES),
        name="gates",
    )(query_slab, key_slab, value_slab, cotangent, gains, *came)


def solution(mesh):
    C, T = mesh.shape["context"], mesh.shape["tensor"]
    slab = P("tensor", "context")
    return jax.shard_map(
        functools.partial(per_device, C, T),
        mesh=mesh,
        in_specs=(slab, slab, slab, slab, slab, P("tensor")),
        out_specs=(slab, slab, slab, slab, slab),
        check_vma=False,
    )
```

```python
import functools
import math

import jax
import jax.numpy as jnp
from jax import lax
from jax.experimental import pallas as pl
from jax.experimental.pallas import tpu as pltpu
from jax.sharding import PartitionSpec as P

MESH = pl.DeviceIdType.MESH
F32 = jnp.float32
BF16 = jnp.bfloat16
LANES = 128
VMEM_BYTES = 62 * 1024 * 1024
UNROLL = 8
OWN = 8


def exchange(lanes=LANES):
    row = lax.broadcasted_iota(jnp.int32, (lanes, lanes), 0)
    col = lax.broadcasted_iota(jnp.int32, (lanes, lanes), 1)
    return (row + col == lanes - 1).astype(BF16)


def far(i, n):
    return n // 2 + ((i + 1) // 2) * (1 - 2 * (i % 2))


def kernel(
    C, T,
    q_hbm, k_hbm, v_hbm, c_hbm, f_hbm,
    back_hbm, grads_hbm,
    q_ref, k_ref, v_ref, c_ref, f_ref,
    fsend, frecv, msend, mrecv, toep, z2, acc, gcat, bsend,
    raw, raw_other, gsend, tsend, trecv,
    load_sem, send_sem, recv_sem,
):
    me = lax.axis_index("context")
    ten = lax.axis_index("tensor")
    half = C // 2
    Z, Y = 4, C // 8
    pair = me // 2
    z = pair // Y
    y = pair % Y
    core = me % 2
    rows = C * OWN

    loads = [
        pltpu.make_async_copy(src, dst, load_sem.at[n])
        for n, (src, dst) in enumerate(
            [(f_hbm, f_ref), (k_hbm, k_ref), (v_hbm, v_ref), (q_hbm, q_ref), (c_hbm, c_ref)]
        )
    ]
    for load in loads:
        load.start()

    def each_peer(start, cores=2):
        columns = []
        for j in range(Z):
            plane = lax.rem(z + far(j, Z), Z)
            columns += [2 * Y * plane + 1 - core, 2 * Y * plane + core][2 - cores :]
        ring(start, columns, False)

    def ring(start, columns, last):
        def at(i, _):
            place = 2 * lax.rem(y + far(i, Y), Y)
            for column in columns:
                start(column + place)
            return 0

        lax.fori_loop(0, Y - 1, at, 0)
        for column in columns[:-1]:
            start(column + 2 * y)
        if last is not False:
            pl.when(last)(lambda: start(columns[-1] + 2 * y))

    def half_peers(start, late, cores=2):
        one = lax.rem((z + 1) // 2 + 1 - late, 2)
        columns = []
        for plane in (2 * late + one, 2 * late + 1 - one):
            columns += [2 * Y * plane + 1 - core, 2 * Y * plane + core][2 - cores :]
        ring(start, columns, z // 2 != late)

    barrier = pltpu.get_barrier_semaphore()
    each_peer(lambda to: pl.semaphore_signal(barrier, inc=1, device_id=(to, ten), device_id_type=MESH))
    for k in range(1, T):
        pl.semaphore_signal(barrier, inc=1, device_id=(me, lax.rem(ten + k, T)), device_id_type=MESH)

    flip = exchange()

    loads[0].wait()
    taps = jnp.dot(f_ref[...], flip, preferred_element_type=F32)
    for r in range(half):
        fsend[r] = taps[r : r + 1]

    for load in loads[1:5]:
        load.wait()
    product = (k_ref[...].astype(F32) * v_ref[...].astype(F32)).astype(BF16)
    mirrored = jnp.dot(product, flip, preferred_element_type=F32).reshape(C, OWN, LANES)
    gmix = (q_ref[...].astype(F32) * c_ref[...].astype(F32)).reshape(C, OWN, LANES)
    msend[...] = jnp.concatenate([mirrored, gmix], axis=1).astype(BF16)

    pl.semaphore_wait(barrier, C - 1 + T - 1)

    def send(src, dst, phase, peer):
        return pltpu.make_async_remote_copy(
            src_ref=src, dst_ref=dst, send_sem=send_sem.at[phase], recv_sem=recv_sem.at[phase],
            device_id=peer, device_id_type=MESH,
        )

    each_peer(lambda to: send(fsend.at[to // 2], frecv.at[core, pair], 0, (to, ten)).start(), cores=1)

    def send_main(to):
        send(msend.at[to], mrecv.at[me], 1, (to, ten)).start()

    each_peer(send_main)

    frecv[core, pair] = fsend[pair]
    mrecv[me] = msend[me]
    toep[0] = jnp.zeros((LANES, LANES), BF16)
    z2[half * 16 :, :] = jnp.zeros((z2.shape[0] - half * 16, 2 * LANES), BF16)
    gcat[rows:, :] = jnp.zeros((gcat.shape[0] - rows, 2 * LANES), BF16)

    row = lax.broadcasted_iota(jnp.int32, (LANES, LANES), 0)
    col = lax.broadcasted_iota(jnp.int32, (LANES, LANES), 1)
    lower = col <= row

    def skew(block):
        return pltpu.roll(block, 1, 1, stride=1, stride_axis=0)

    other = me + 1 - 2 * core
    some_taps = frecv.at[core, pl.ds(0, half - 1)]
    send(some_taps, some_taps, 0, (me, ten)).wait_recv()
    tap_swap = send(frecv.at[core], frecv.at[core], 6, (other, ten))
    tap_swap.start()

    tap_swap.wait_recv()
    def build(n, last):
        for u in range(UNROLL):
            d = UNROLL * n + u
            turned = skew(jnp.broadcast_to(frecv[u % 2, d // 2], (LANES, LANES)))
            toep[d + 1] = jnp.where(lower, turned, last).astype(BF16)
            last = turned
        return last

    lax.fori_loop(0, C // UNROLL, build, jnp.zeros((LANES, LANES), F32))

    send(mrecv.at[pl.ds(0, C - 1)], mrecv.at[pl.ds(0, C - 1)], 1, (me, ten)).wait_recv()
    zero = jnp.zeros((OWN, LANES), F32)
    whole = mrecv[...].astype(F32)
    xt = whole[:, :OWN].reshape(rows, LANES).T.astype(BF16)
    gpart = whole[:, OWN:]
    after = jnp.concatenate([gpart[1:], zero[None]], axis=0)
    gcat[0:rows, :] = jnp.concatenate([gpart, after], axis=2).reshape(rows, 2 * LANES).astype(BF16)

    def lags(e, depth):
        first = pl.multiple_of(16 * e, 16)
        return jnp.dot(xt[:, :depth], gcat[pl.ds(first, depth), :], preferred_element_type=F32)

    def gather(depth, group):
        def body(n, last):
            parts = [lags(group * n + u, depth) for u in range(group)]
            for u in reversed(range(group)):
                for side in (1, 0):
                    turned = skew(parts[u][:, side * LANES : (side + 1) * LANES])
                    place = 2 * (group * n + u) + side
                    raw[place] = jnp.sum(jnp.where(lower, turned, last), axis=0, keepdims=True)
                    last = turned
            return last

        return body

    group = min(8, half // 2)
    last = jnp.zeros((LANES, LANES), F32)
    for n in reversed(range(half // group)):
        depth = rows if 2 * group * n < half else rows // 2
        last = gather(depth, group)(n, last)

    swap = send(raw, raw_other, 3, (other, ten))
    swap.start()

    for j in range(half):
        two = []
        for i in (2 * j, 2 * j + 1):
            two.append(jnp.concatenate([mrecv[C - 1 - i].astype(F32)[:OWN], mrecv[i].astype(F32)[OWN:]], axis=0))
        z2[16 * j : 16 * j + 16, :] = jnp.concatenate(two, axis=1).astype(BF16)

    swap.wait_recv()
    total = raw[...] + raw_other[...]
    size = jnp.broadcast_to(jnp.sum(jnp.sum(total * total, axis=0), axis=1, keepdims=True), (1, LANES))
    tsend[...] = size
    trecv[ten] = size
    for k in range(1, T):
        send(tsend, trecv.at[ten], 5, (me, lax.rem(ten + k, T))).start()

    def weight(d):
        top = jnp.concatenate([toep[2 * d + 1], toep[2 * d]], axis=1)
        low = jnp.concatenate([toep[2 * d + 2], toep[2 * d + 1]], axis=1)
        return jnp.concatenate([top, low], axis=0)

    step = min(4, half)
    for d0 in range(0, half, step):
        size = 16 * (half - d0)
        left = jnp.concatenate([z2[16 * (d0 + u) : 16 * (d0 + u) + size, :] for u in range(step)], axis=1)
        right = jnp.concatenate([weight(d0 + u) for u in range(step)], axis=0)
        part = jnp.dot(left, right, preferred_element_type=F32)
        if d0 == 0:
            acc[...] = part
        else:
            acc[0:size, :] += part

    for i in range(C):
        m = C - 1 - i
        conv = acc[16 * (m // 2) : 16 * (m // 2) + OWN, (m % 2) * LANES : (m % 2 + 1) * LANES]
        corr = acc[16 * (i // 2) + OWN : 16 * (i // 2) + 16, (i % 2) * LANES : (i % 2 + 1) * LANES]
        bsend[i] = jnp.concatenate([conv, corr], axis=0).astype(BF16)

    def send_back(to):
        send(bsend.at[to], back_hbm.at[me], 2, (to, ten)).start()

    def send_grad(to):
        send(gsend.at[to], grads_hbm.at[pair], 4, (to, ten)).start()

    half_peers(send_back, 0)

    if T > 1:
        part = pl.ds(0, T - 1)
        send(trecv.at[part], trecv.at[part], 5, (me, ten)).wait_recv()
    square = jnp.sum(trecv[...], axis=0)
    for i in range(C):
        gsend[i] = jnp.concatenate([raw[i] + raw_other[i], square], axis=0)
    half_peers(send_grad, 0, cores=1)
    half_peers(send_back, 1)
    half_peers(send_grad, 1, cores=1)
    own_back = pltpu.make_async_copy(bsend.at[me], back_hbm.at[me], load_sem.at[0])
    own_grad = pltpu.make_async_copy(gsend.at[me], grads_hbm.at[pair], load_sem.at[1])
    own_back.start()
    own_grad.start()

    some_back = back_hbm.at[pl.ds(0, C - 1)]
    send(some_back, some_back, 2, (me, ten)).wait_recv()
    some_grads = grads_hbm.at[pl.ds(0, half - 1)]
    send(some_grads, some_grads, 4, (me, ten)).wait_recv()
    own_back.wait()
    own_grad.wait()

    send(some_taps, some_taps, 0, (me, ten)).wait_send()
    tap_swap.wait_send()
    send(msend.at[pl.ds(0, C - 1)], msend.at[pl.ds(0, C - 1)], 1, (me, ten)).wait_send()
    send(bsend.at[pl.ds(0, C - 1)], bsend.at[pl.ds(0, C - 1)], 2, (me, ten)).wait_send()
    swap.wait_send()

    send(some_grads, some_grads, 4, (me, ten)).wait_send()
    if T > 1:
        part = pl.ds(0, T - 1)
        send(trecv.at[part], trecv.at[part], 5, (me, ten)).wait_send()


def gates(
    C, entries,
    q_hbm, k_hbm, v_hbm, c_hbm, gain_hbm, back_hbm, grads_hbm,
    mixed_hbm, gq_hbm, gk_hbm, gv_hbm, fg_hbm,
    q_ref, k_ref, v_ref, c_ref, gain_ref, back, grads,
    mixed, gq, gk, gv, fg, gain_col, load_sem, store_sem,
):
    half = C // 2
    rows = C * OWN
    pairs = [
        (q_hbm, q_ref), (k_hbm, k_ref), (v_hbm, v_ref), (c_hbm, c_ref), (back_hbm, back),
        (gain_hbm, gain_ref), (grads_hbm, grads),
    ]
    loads = [pltpu.make_async_copy(src, dst, load_sem.at[n]) for n, (src, dst) in enumerate(pairs)]
    for load in loads:
        load.start()
    outs = [(mixed, mixed_hbm), (gq, gq_hbm), (gk, gk_hbm), (gv, gv_hbm), (fg, fg_hbm)]
    stores = [pltpu.make_async_copy(src, dst, store_sem.at[n]) for n, (src, dst) in enumerate(outs)]
    flip = exchange()
    for load in loads:
        load.wait()

    for n in range(rows // LANES):
        wide = jnp.broadcast_to(gain_ref[n : n + 1, :], (LANES, LANES))
        gain_col[n * LANES : (n + 1) * LANES, :] = wide.T
    gain = gain_col[...]
    both = back[...].astype(F32)
    conv = jnp.dot(both[:, :OWN].reshape(rows, LANES).astype(BF16), flip, preferred_element_type=F32)
    corr = both[:, OWN:].reshape(rows, LANES)
    kf = k_ref[...].astype(F32)
    vf = v_ref[...].astype(F32)
    qf = q_ref[...].astype(F32)
    cf = c_ref[...].astype(F32)
    backward = corr + gain * (qf * cf).astype(BF16).astype(F32)
    gk[...] = (backward * vf).astype(BF16)
    stores[2].start()
    gv[...] = (backward * kf).astype(BF16)
    stores[3].start()
    forward = conv + gain * (kf * vf).astype(BF16).astype(F32)
    mixed[...] = (qf * forward).astype(BF16)
    stores[0].start()
    gq[...] = (cf * forward).astype(BF16)
    stores[1].start()

    squared = jnp.sum(grads[:, 1:2, :], axis=0)
    factor = jnp.minimum(1.0, math.sqrt(entries) / jnp.sqrt(squared + 1e-6))
    for r in range(half):
        fg[r : r + 1, :] = grads[r, 0:1, :] * factor
    stores[4].start()
    for store in stores:
        store.wait()


def per_device(C, T, query_slab, key_slab, value_slab, cotangent, filters, skip_gain):
    channels, tokens = query_slab.shape
    half = C // 2
    rows = C * OWN
    entries = half * T * tokens * C
    gains = skip_gain.reshape(channels // LANES, LANES)
    hbm_spec = pl.BlockSpec(memory_space=pltpu.HBM)
    back = jax.ShapeDtypeStruct((C, 16, LANES), BF16)
    grads = jax.ShapeDtypeStruct((half, 2, LANES), F32)
    came = pl.pallas_call(
        functools.partial(kernel, C, T),
        out_shape=(back, grads),
        in_specs=[hbm_spec] * 5,
        out_specs=(hbm_spec,) * 2,
        scratch_shapes=[
            pltpu.VMEM((channels, tokens), BF16),
            pltpu.VMEM((channels, tokens), BF16),
            pltpu.VMEM((channels, tokens), BF16),
            pltpu.VMEM((channels, tokens), BF16),
            pltpu.VMEM((half, tokens), BF16),
            pltpu.VMEM((half, 1, LANES), F32),
            pltpu.VMEM((2, half, 1, LANES), F32),
            pltpu.VMEM((C, 16, LANES), BF16),
            pltpu.VMEM((C, 16, LANES), BF16),
            pltpu.VMEM((C + 1, LANES, LANES), BF16),
            pltpu.VMEM((16 * (half + 4), 2 * LANES), BF16),
            pltpu.VMEM((16 * half, 2 * LANES), F32),
            pltpu.VMEM((2 * rows, 2 * LANES), BF16),
            pltpu.VMEM((C, 16, LANES), BF16),
            pltpu.VMEM((C, 1, LANES), F32),
            pltpu.VMEM((C, 1, LANES), F32),
            pltpu.VMEM((C, 2, LANES), F32),
            pltpu.VMEM((1, LANES), F32),
            pltpu.VMEM((T, 1, LANES), F32),
            pltpu.SemaphoreType.DMA((7,)),
            pltpu.SemaphoreType.DMA((7,)),
            pltpu.SemaphoreType.DMA((7,)),
        ],
        compiler_params=pltpu.CompilerParams(
            collective_id=0, has_side_effects=True, vmem_limit_bytes=VMEM_BYTES
        ),
        name="hyena",
    )(query_slab, key_slab, value_slab, cotangent, filters)
    slab = jax.ShapeDtypeStruct((channels, tokens), BF16)
    slab_buffer = pltpu.VMEM((channels, tokens), BF16)
    return pl.pallas_call(
        functools.partial(gates, C, entries),
        out_shape=(slab, slab, slab, slab, jax.ShapeDtypeStruct((half, tokens), F32)),
        in_specs=[hbm_spec] * 7,
        out_specs=(hbm_spec,) * 5,
        scratch_shapes=[
            slab_buffer, slab_buffer, slab_buffer, slab_buffer,
            pltpu.VMEM(gains.shape, F32),
            pltpu.VMEM(back.shape, BF16),
            pltpu.VMEM(grads.shape, F32),
            slab_buffer, slab_buffer, slab_buffer, slab_buffer,
            pltpu.VMEM((half, tokens), F32),
            pltpu.VMEM((channels, LANES), F32),
            pltpu.SemaphoreType.DMA((7,)),
            pltpu.SemaphoreType.DMA((5,)),
        ],
        compiler_params=pltpu.CompilerParams(vmem_limit_bytes=VMEM_BYTES),
        name="gates",
    )(query_slab, key_slab, value_slab, cotangent, gains, *came)


def solution(mesh):
    C, T = mesh.shape["context"], mesh.shape["tensor"]
    slab = P("tensor", "context")
    return jax.shard_map(
        functools.partial(per_device, C, T),
        mesh=mesh,
        in_specs=(slab, slab, slab, slab, slab, P("tensor")),
        out_specs=(slab, slab, slab, slab, slab),
        check_vma=False,
    )
```

```python
import functools
import math

import jax
import jax.numpy as jnp
from jax import lax
from jax.experimental import pallas as pl
from jax.experimental.pallas import tpu as pltpu
from jax.sharding import PartitionSpec as P

MESH = pl.DeviceIdType.MESH
F32 = jnp.float32
BF16 = jnp.bfloat16
LANES = 128
VMEM_BYTES = 32 * 1024 * 1024
UNROLL = 8
OWN = 8


def exchange(lanes=LANES):
    row = lax.broadcasted_iota(jnp.int32, (lanes, lanes), 0)
    col = lax.broadcasted_iota(jnp.int32, (lanes, lanes), 1)
    return (row + col == lanes - 1).astype(BF16)


def far(i, n):
    return n // 2 + ((i + 1) // 2) * (1 - 2 * (i % 2))


def kernel(
    C, T,
    q_hbm, k_hbm, v_hbm, c_hbm, f_hbm, gain_hbm,
    back, grads, sizes, q_ref, k_ref, v_ref, c_ref, scaled_product, scaled_gmix,
    f_ref, gain_ref,
    fsend, frecv, msend, mrecv, toep, z2, acc, gcat, bsend,
    raw, raw_other, gsend, tsend,
    load_sem, send_sem, recv_sem,
):
    me = lax.axis_index("context")
    ten = lax.axis_index("tensor")
    half = C // 2
    Z, Y = 4, C // 8
    pair = me // 2
    z = pair // Y
    y = pair % Y
    core = me % 2
    rows = C * OWN

    def each_peer(start, cores=2):
        columns = []
        for j in range(Z):
            plane = lax.rem(z + far(j, Z), Z)
            columns += [2 * Y * plane + 1 - core, 2 * Y * plane + core][2 - cores :]
        ring(start, columns, False)

    def ring(start, columns, last):
        def at(i, _):
            place = 2 * lax.rem(y + far(i, Y), Y)
            for column in columns:
                start(column + place)
            return 0

        lax.fori_loop(0, Y - 1, at, 0)
        for column in columns[:-1]:
            start(column + 2 * y)
        if last is not False:
            pl.when(last)(lambda: start(columns[-1] + 2 * y))

    def half_peers(start, late, cores=2):
        one = lax.rem((z + 1) // 2 + 1 - late, 2)
        columns = []
        for plane in (2 * late + one, 2 * late + 1 - one):
            columns += [2 * Y * plane + 1 - core, 2 * Y * plane + core][2 - cores :]
        ring(start, columns, z // 2 != late)

    barrier = pltpu.get_barrier_semaphore()
    each_peer(lambda to: pl.semaphore_signal(barrier, inc=1, device_id=(to, ten), device_id_type=MESH))
    for k in range(1, T):
        pl.semaphore_signal(barrier, inc=1, device_id=(me, lax.rem(ten + k, T)), device_id_type=MESH)

    loads = [
        pltpu.make_async_copy(src, dst, load_sem.at[n])
        for n, (src, dst) in enumerate(
            [(f_hbm, f_ref), (k_hbm, k_ref), (v_hbm, v_ref), (q_hbm, q_ref), (c_hbm, c_ref), (gain_hbm, gain_ref)]
        )
    ]
    for load in loads:
        load.start()

    flip = exchange()

    loads[0].wait()
    taps = jnp.dot(f_ref[...], flip, preferred_element_type=F32)
    for r in range(half):
        fsend[r] = taps[r : r + 1]

    for load in loads[1:5]:
        load.wait()
    product = (k_ref[...].astype(F32) * v_ref[...].astype(F32)).astype(BF16)
    mirrored = jnp.dot(product, flip, preferred_element_type=F32).reshape(C, OWN, LANES)
    gmix = (q_ref[...].astype(F32) * c_ref[...].astype(F32)).reshape(C, OWN, LANES)
    msend[...] = jnp.concatenate([mirrored, gmix], axis=1).astype(BF16)

    pl.semaphore_wait(barrier, C - 1 + T - 1)

    def send(src, dst, phase, peer):
        return pltpu.make_async_remote_copy(
            src_ref=src, dst_ref=dst, send_sem=send_sem.at[phase], recv_sem=recv_sem.at[phase],
            device_id=peer, device_id_type=MESH,
        )

    def send_main(to):
        send(msend.at[to], mrecv.at[me], 1, (to, ten)).start()

    def send_taps(to):
        send(fsend.at[to // 2], frecv.at[core, pair], 0, (to, ten)).start()

    each_peer(send_taps, cores=1)
    each_peer(send_main)

    frecv[core, pair] = fsend[pair]
    mrecv[me] = msend[me]
    loads[5].wait()
    for n in range(rows // LANES):
        lines = slice(n * LANES, (n + 1) * LANES)
        gain = jnp.broadcast_to(gain_ref[n : n + 1, :], (LANES, LANES)).T
        part = (k_ref[lines].astype(F32) * v_ref[lines].astype(F32)).astype(BF16)
        scaled_product[lines] = gain * part.astype(F32)
        part = (q_ref[lines].astype(F32) * c_ref[lines].astype(F32)).astype(BF16)
        scaled_gmix[lines] = gain * part.astype(F32)
    toep[0] = jnp.zeros((LANES, LANES), BF16)
    z2[half * 16 :, :] = jnp.zeros((z2.shape[0] - half * 16, 2 * LANES), BF16)
    gcat[rows:, :] = jnp.zeros((gcat.shape[0] - rows, 2 * LANES), BF16)

    row = lax.broadcasted_iota(jnp.int32, (LANES, LANES), 0)
    col = lax.broadcasted_iota(jnp.int32, (LANES, LANES), 1)
    lower = col <= row

    def skew(block):
        return pltpu.roll(block, 1, 1, stride=1, stride_axis=0)

    other = me + 1 - 2 * core
    some_taps = frecv.at[core, pl.ds(0, half - 1)]
    send(some_taps, some_taps, 0, (me, ten)).wait_recv()
    tap_swap = send(frecv.at[core], frecv.at[core], 6, (other, ten))
    tap_swap.start()

    tap_swap.wait_recv()
    def build(n, last):
        for u in range(UNROLL):
            d = UNROLL * n + u
            turned = skew(jnp.broadcast_to(frecv[u % 2, d // 2], (LANES, LANES)))
            toep[d + 1] = jnp.where(lower, turned, last).astype(BF16)
            last = turned
        return last

    lax.fori_loop(0, C // UNROLL, build, jnp.zeros((LANES, LANES), F32))

    send(mrecv.at[pl.ds(0, C - 1)], mrecv.at[pl.ds(0, C - 1)], 1, (me, ten)).wait_recv()
    zero = jnp.zeros((OWN, LANES), F32)
    whole = mrecv[...].astype(F32)
    xt = whole[:, :OWN].reshape(rows, LANES).T.astype(BF16)
    gpart = whole[:, OWN:]
    after = jnp.concatenate([gpart[1:], zero[None]], axis=0)
    gcat[0:rows, :] = jnp.concatenate([gpart, after], axis=2).reshape(rows, 2 * LANES).astype(BF16)

    def lags(e, depth):
        first = pl.multiple_of(16 * e, 16)
        return jnp.dot(xt[:, :depth], gcat[pl.ds(first, depth), :], preferred_element_type=F32)

    def gather(depth, group):
        def body(n, last):
            parts = [lags(group * n + u, depth) for u in range(group)]
            for u in reversed(range(group)):
                for side in (1, 0):
                    turned = skew(parts[u][:, side * LANES : (side + 1) * LANES])
                    place = 2 * (group * n + u) + side
                    raw[place] = jnp.sum(jnp.where(lower, turned, last), axis=0, keepdims=True)
                    last = turned
            return last

        return body

    group = min(8, half // 2)
    last = jnp.zeros((LANES, LANES), F32)
    for n in reversed(range(half // group)):
        depth = rows if 2 * group * n < half else rows // 2
        last = gather(depth, group)(n, last)

    swap = send(raw, raw_other, 3, (other, ten))
    swap.start()

    for j in range(half):
        two = []
        for i in (2 * j, 2 * j + 1):
            two.append(jnp.concatenate([mrecv[C - 1 - i].astype(F32)[:OWN], mrecv[i].astype(F32)[OWN:]], axis=0))
        z2[16 * j : 16 * j + 16, :] = jnp.concatenate(two, axis=1).astype(BF16)

    swap.wait_recv()
    total = raw[...] + raw_other[...]
    size = jnp.broadcast_to(jnp.sum(jnp.sum(total * total, axis=0), axis=1, keepdims=True), (1, LANES))
    gsend[:, 0:1, :] = total
    gsend[:, 1:2, :] = jnp.broadcast_to(size[None], (C, 1, LANES))

    def send_grad(to):
        send(gsend.at[to], grads.at[pair], 4, (to, ten)).start()

    half_peers(send_grad, 0, cores=1)
    grads[pair] = gsend[me]

    def weight(d):
        top = jnp.concatenate([toep[2 * d + 1], toep[2 * d]], axis=1)
        low = jnp.concatenate([toep[2 * d + 2], toep[2 * d + 1]], axis=1)
        return jnp.concatenate([top, low], axis=0)

    step = min(4, half)
    for d0 in range(0, half, step):
        size = 16 * (half - d0)
        left = jnp.concatenate([z2[16 * (d0 + u) : 16 * (d0 + u) + size, :] for u in range(step)], axis=1)
        right = jnp.concatenate([weight(d0 + u) for u in range(step)], axis=0)
        part = jnp.dot(left, right, preferred_element_type=F32)
        if d0 == 0:
            acc[...] = part
        else:
            acc[0:size, :] += part

    for i in range(C):
        m = C - 1 - i
        conv = acc[16 * (m // 2) : 16 * (m // 2) + OWN, (m % 2) * LANES : (m % 2 + 1) * LANES]
        corr = acc[16 * (i // 2) + OWN : 16 * (i // 2) + 16, (i % 2) * LANES : (i % 2 + 1) * LANES]
        bsend[i] = jnp.concatenate([conv, corr], axis=0).astype(BF16)

    def send_back(to):
        send(bsend.at[to], back.at[me], 2, (to, ten)).start()

    half_peers(send_back, 0)
    half_peers(send_grad, 1, cores=1)
    half_peers(send_back, 1)
    back[me] = bsend[me]

    some_grads = grads.at[pl.ds(0, half - 1)]
    send(some_grads, some_grads, 4, (me, ten)).wait_recv()
    square = jnp.sum(grads[:, 1:2, :], axis=0)
    tsend[...] = square
    for k in range(1, T):
        send(tsend, sizes.at[ten], 5, (me, lax.rem(ten + k, T))).start()
    sizes[ten] = square

    some_back = back.at[pl.ds(0, C - 1)]
    send(some_back, some_back, 2, (me, ten)).wait_recv()
    if T > 1:
        part = pl.ds(0, T - 1)
        send(sizes.at[part], sizes.at[part], 5, (me, ten)).wait_recv()

    send(some_taps, some_taps, 0, (me, ten)).wait_send()
    tap_swap.wait_send()
    send(msend.at[pl.ds(0, C - 1)], msend.at[pl.ds(0, C - 1)], 1, (me, ten)).wait_send()
    send(bsend.at[pl.ds(0, C - 1)], bsend.at[pl.ds(0, C - 1)], 2, (me, ten)).wait_send()
    swap.wait_send()

    send(some_grads, some_grads, 4, (me, ten)).wait_send()
    if T > 1:
        part = pl.ds(0, T - 1)
        send(sizes.at[part], sizes.at[part], 5, (me, ten)).wait_send()


def gates(
    C, entries,
    back, grads, sizes, q_ref, k_ref, v_ref, c_ref, scaled_product, scaled_gmix,
    mixed_hbm, gq_hbm, gk_hbm, gv_hbm, fg_hbm,
    mixed, gq, gk, gv, fg, store_sem,
):
    half = C // 2
    rows = C * OWN
    outs = [(mixed, mixed_hbm), (gq, gq_hbm), (gk, gk_hbm), (gv, gv_hbm), (fg, fg_hbm)]
    stores = [pltpu.make_async_copy(src, dst, store_sem.at[n]) for n, (src, dst) in enumerate(outs)]
    both = back[...].astype(F32)
    backward = both[:, OWN:].reshape(rows, LANES) + scaled_gmix[...]
    gk[...] = (backward * v_ref[...].astype(F32)).astype(BF16)
    stores[2].start()
    gv[...] = (backward * k_ref[...].astype(F32)).astype(BF16)
    stores[3].start()
    conv = jnp.dot(both[:, :OWN].reshape(rows, LANES).astype(BF16), exchange(), preferred_element_type=F32)
    forward = conv + scaled_product[...]
    mixed[...] = (q_ref[...].astype(F32) * forward).astype(BF16)
    stores[0].start()
    gq[...] = (c_ref[...].astype(F32) * forward).astype(BF16)
    stores[1].start()

    squared = jnp.sum(sizes[...], axis=0)
    factor = jnp.minimum(1.0, math.sqrt(entries) / jnp.sqrt(squared + 1e-6))
    for r in range(half):
        fg[r : r + 1, :] = grads[r, 0:1, :] * factor
    stores[4].start()
    for store in stores:
        store.wait()


def per_device(C, T, query_slab, key_slab, value_slab, cotangent, filters, skip_gain):
    channels, tokens = query_slab.shape
    half = C // 2
    rows = C * OWN
    entries = half * T * tokens * C
    gains = skip_gain.reshape(channels // LANES, LANES)
    hbm_spec = pl.BlockSpec(memory_space=pltpu.HBM)
    slab = jax.ShapeDtypeStruct((channels, tokens), BF16)
    kept_slab = pltpu.VMEM((channels, tokens), BF16)
    kept_scaled = pltpu.VMEM((channels, tokens), F32)
    vmem_spec = pl.BlockSpec(memory_space=pltpu.VMEM)
    inputs = (query_slab, key_slab, value_slab, cotangent, filters, gains)
    kept = pl.pallas_call(
        functools.partial(kernel, C, T),
        out_shape=(
            pltpu.VMEM((C, 16, LANES), BF16),
            pltpu.VMEM((half, 2, LANES), F32),
            pltpu.VMEM((T, 1, LANES), F32),
            kept_slab, kept_slab, kept_slab, kept_slab, kept_scaled, kept_scaled,
        ),
        in_specs=[hbm_spec] * 6,
        out_specs=(vmem_spec,) * 9,
        scratch_shapes=[
            pltpu.VMEM((half, tokens), BF16),
            pltpu.VMEM(gains.shape, F32),
            pltpu.VMEM((half, 1, LANES), F32),
            pltpu.VMEM((2, half, 1, LANES), F32),
            pltpu.VMEM((C, 16, LANES), BF16),
            pltpu.VMEM((C, 16, LANES), BF16),
            pltpu.VMEM((C + 1, LANES, LANES), BF16),
            pltpu.VMEM((16 * (half + 4), 2 * LANES), BF16),
            pltpu.VMEM((16 * half, 2 * LANES), F32),
            pltpu.VMEM((2 * rows, 2 * LANES), BF16),
            pltpu.VMEM((C, 16, LANES), BF16),
            pltpu.VMEM((C, 1, LANES), F32),
            pltpu.VMEM((C, 1, LANES), F32),
            pltpu.VMEM((C, 2, LANES), F32),
            pltpu.VMEM((1, LANES), F32),
            pltpu.SemaphoreType.DMA((7,)),
            pltpu.SemaphoreType.DMA((7,)),
            pltpu.SemaphoreType.DMA((7,)),
        ],
        compiler_params=pltpu.CompilerParams(
            collective_id=0, has_side_effects=True, vmem_limit_bytes=VMEM_BYTES
        ),
        name="hyena",
    )(*(pltpu.with_memory_space_constraint(array, pltpu.HBM) for array in inputs))
    slab_buffer = pltpu.VMEM((channels, tokens), BF16)
    return pl.pallas_call(
        functools.partial(gates, C, entries),
        out_shape=(slab, slab, slab, slab, jax.ShapeDtypeStruct((half, tokens), F32)),
        in_specs=[vmem_spec] * 9,
        out_specs=(hbm_spec,) * 5,
        scratch_shapes=[
            slab_buffer, slab_buffer, slab_buffer, slab_buffer,
            pltpu.VMEM((half, tokens), F32),
            pltpu.SemaphoreType.DMA((5,)),
        ],
        compiler_params=pltpu.CompilerParams(vmem_limit_bytes=VMEM_BYTES),
        name="gates",
    )(*(pltpu.with_memory_space_constraint(array, pltpu.VMEM) for array in kept))


def solution(mesh):
    C, T = mesh.shape["context"], mesh.shape["tensor"]
    slab = P("tensor", "context")
    return jax.shard_map(
        functools.partial(per_device, C, T),
        mesh=mesh,
        in_specs=(slab, slab, slab, slab, slab, P("tensor")),
        out_specs=(slab, slab, slab, slab, slab),
        check_vma=False,
    )
```

```python
import functools
import math

import jax
import jax.numpy as jnp
from jax import lax
from jax.experimental import pallas as pl
from jax.experimental.pallas import tpu as pltpu
from jax.sharding import PartitionSpec as P

MESH = pl.DeviceIdType.MESH
F32 = jnp.float32
BF16 = jnp.bfloat16
LANES = 128
VMEM_BYTES = 32 * 1024 * 1024
UNROLL = 16
OWN = 8


def exchange(lanes=LANES):
    row = lax.broadcasted_iota(jnp.int32, (lanes, lanes), 0)
    col = lax.broadcasted_iota(jnp.int32, (lanes, lanes), 1)
    return (row + col == lanes - 1).astype(BF16)


def far(i, n):
    return n // 2 + ((i + 1) // 2) * (1 - 2 * (i % 2))


def kernel(
    C, T,
    q_hbm, k_hbm, v_hbm, c_hbm, f_hbm, gain_hbm,
    back, grads, sizes, q_ref, k_ref, v_ref, c_ref, scaled_product, scaled_gmix,
    f_ref, gain_ref,
    fsend, frecv, msend, mrecv, toep, z2, acc, gcat, bsend,
    raw, raw_other, gsend, tsend,
    load_sem, send_sem, recv_sem,
):
    me = lax.axis_index("context")
    ten = lax.axis_index("tensor")
    half = C // 2
    Z, Y = 4, C // 8
    pair = me // 2
    z = pair // Y
    y = pair % Y
    core = me % 2
    rows = C * OWN

    def each_peer(start, cores=2):
        columns = []
        for j in range(Z):
            plane = lax.rem(z + far(j, Z), Z)
            columns += [2 * Y * plane + 1 - core, 2 * Y * plane + core][2 - cores :]
        ring(start, columns, False)

    def ring(start, columns, last):
        def at(i, _):
            place = 2 * lax.rem(y + far(i, Y), Y)
            for column in columns:
                start(column + place)
            return 0

        lax.fori_loop(0, Y - 1, at, 0)
        for column in columns[:-1]:
            start(column + 2 * y)
        if last is not False:
            pl.when(last)(lambda: start(columns[-1] + 2 * y))

    def half_peers(start, late, cores=2):
        one = lax.rem((z + 1) // 2 + 1 - late, 2)
        columns = []
        for plane in (2 * late + one, 2 * late + 1 - one):
            columns += [2 * Y * plane + 1 - core, 2 * Y * plane + core][2 - cores :]
        ring(start, columns, z // 2 != late)

    barrier = pltpu.get_barrier_semaphore()
    each_peer(lambda to: pl.semaphore_signal(barrier, inc=1, device_id=(to, ten), device_id_type=MESH))
    for k in range(1, T):
        pl.semaphore_signal(barrier, inc=1, device_id=(me, lax.rem(ten + k, T)), device_id_type=MESH)

    loads = [
        pltpu.make_async_copy(src, dst, load_sem.at[n])
        for n, (src, dst) in enumerate(
            [(f_hbm, f_ref), (k_hbm, k_ref), (v_hbm, v_ref), (q_hbm, q_ref), (c_hbm, c_ref), (gain_hbm, gain_ref)]
        )
    ]
    for load in loads:
        load.start()

    flip = exchange()

    loads[0].wait()
    taps = jnp.dot(f_ref[...], flip, preferred_element_type=F32)
    for r in range(half):
        fsend[r] = taps[r : r + 1]

    for load in loads[1:5]:
        load.wait()
    product = (k_ref[...].astype(F32) * v_ref[...].astype(F32)).astype(BF16)
    mirrored = jnp.dot(product, flip, preferred_element_type=F32).reshape(C, OWN, LANES)
    gmix = (q_ref[...].astype(F32) * c_ref[...].astype(F32)).reshape(C, OWN, LANES)
    msend[...] = jnp.concatenate([mirrored, gmix], axis=1).astype(BF16)

    pl.semaphore_wait(barrier, C - 1 + T - 1)

    def send(src, dst, phase, peer):
        return pltpu.make_async_remote_copy(
            src_ref=src, dst_ref=dst, send_sem=send_sem.at[phase], recv_sem=recv_sem.at[phase],
            device_id=peer, device_id_type=MESH,
        )

    def send_main(to):
        send(msend.at[to], mrecv.at[me], 1, (to, ten)).start()

    def send_taps(to):
        send(fsend.at[to // 2], frecv.at[core, pair], 0, (to, ten)).start()

    each_peer(send_taps, cores=1)
    each_peer(send_main)

    frecv[core, pair] = fsend[pair]
    mrecv[me] = msend[me]
    loads[5].wait()
    for n in range(rows // LANES):
        lines = slice(n * LANES, (n + 1) * LANES)
        gain = jnp.broadcast_to(gain_ref[n : n + 1, :], (LANES, LANES)).T
        part = (k_ref[lines].astype(F32) * v_ref[lines].astype(F32)).astype(BF16)
        scaled_product[lines] = gain * part.astype(F32)
        part = (q_ref[lines].astype(F32) * c_ref[lines].astype(F32)).astype(BF16)
        scaled_gmix[lines] = gain * part.astype(F32)
    toep[0] = jnp.zeros((LANES, LANES), BF16)
    z2[half * 16 :, :] = jnp.zeros((z2.shape[0] - half * 16, 2 * LANES), BF16)
    gcat[rows:, :] = jnp.zeros((gcat.shape[0] - rows, 2 * LANES), BF16)

    row = lax.broadcasted_iota(jnp.int32, (LANES, LANES), 0)
    col = lax.broadcasted_iota(jnp.int32, (LANES, LANES), 1)
    lower = col <= row

    def skew(block):
        return pltpu.roll(block, 1, 1, stride=1, stride_axis=0)

    other = me + 1 - 2 * core
    some_taps = frecv.at[core, pl.ds(0, half - 1)]
    send(some_taps, some_taps, 0, (me, ten)).wait_recv()
    tap_swap = send(frecv.at[core], frecv.at[core], 6, (other, ten))
    tap_swap.start()

    tap_swap.wait_recv()
    def build(n, last):
        for u in range(UNROLL):
            d = UNROLL * n + u
            turned = skew(jnp.broadcast_to(frecv[u % 2, d // 2], (LANES, LANES)))
            toep[d + 1] = jnp.where(lower, turned, last).astype(BF16)
            last = turned
        return last

    lax.fori_loop(0, C // UNROLL, build, jnp.zeros((LANES, LANES), F32))

    send(mrecv.at[pl.ds(0, C - 1)], mrecv.at[pl.ds(0, C - 1)], 1, (me, ten)).wait_recv()
    zero = jnp.zeros((OWN, LANES), F32)
    whole = mrecv[...].astype(F32)
    xt = whole[:, :OWN].reshape(rows, LANES).T.astype(BF16)
    gpart = whole[:, OWN:]
    after = jnp.concatenate([gpart[1:], zero[None]], axis=0)
    gcat[0:rows, :] = jnp.concatenate([gpart, after], axis=2).reshape(rows, 2 * LANES).astype(BF16)

    def lags(e, depth):
        first = pl.multiple_of(16 * e, 16)
        return jnp.dot(xt[:, :depth], gcat[pl.ds(first, depth), :], preferred_element_type=F32)

    def gather(depth, group):
        def body(n, last):
            parts = [lags(group * n + u, depth) for u in range(group)]
            for u in reversed(range(group)):
                for side in (1, 0):
                    turned = skew(parts[u][:, side * LANES : (side + 1) * LANES])
                    place = 2 * (group * n + u) + side
                    raw[place] = jnp.sum(jnp.where(lower, turned, last), axis=0, keepdims=True)
                    last = turned
            return last

        return body

    group = min(8, half // 2)
    last = jnp.zeros((LANES, LANES), F32)
    for n in reversed(range(half // group)):
        depth = rows if 2 * group * n < half else rows // 2
        last = gather(depth, group)(n, last)

    swap = send(raw, raw_other, 3, (other, ten))
    swap.start()

    for j in range(half):
        two = []
        for i in (2 * j, 2 * j + 1):
            two.append(jnp.concatenate([mrecv[C - 1 - i].astype(F32)[:OWN], mrecv[i].astype(F32)[OWN:]], axis=0))
        z2[16 * j : 16 * j + 16, :] = jnp.concatenate(two, axis=1).astype(BF16)

    swap.wait_recv()
    total = raw[...] + raw_other[...]
    size = jnp.sum(total * total, axis=0)
    gsend[:, 0:1, :] = total
    gsend[:, 1:2, :] = jnp.broadcast_to(size[None], (C, 1, LANES))

    def send_grad(to):
        send(gsend.at[to], grads.at[pair], 4, (to, ten)).start()

    half_peers(send_grad, 0, cores=1)
    grads[pair] = gsend[me]

    def weight(d):
        top = jnp.concatenate([toep[2 * d + 1], toep[2 * d]], axis=1)
        low = jnp.concatenate([toep[2 * d + 2], toep[2 * d + 1]], axis=1)
        return jnp.concatenate([top, low], axis=0)

    step = min(4, half)
    for d0 in range(0, half, step):
        size = 16 * (half - d0)
        left = jnp.concatenate([z2[16 * (d0 + u) : 16 * (d0 + u) + size, :] for u in range(step)], axis=1)
        right = jnp.concatenate([weight(d0 + u) for u in range(step)], axis=0)
        part = jnp.dot(left, right, preferred_element_type=F32)
        if d0 == 0:
            acc[...] = part
        else:
            acc[0:size, :] += part

    for i in range(C):
        m = C - 1 - i
        conv = acc[16 * (m // 2) : 16 * (m // 2) + OWN, (m % 2) * LANES : (m % 2 + 1) * LANES]
        corr = acc[16 * (i // 2) + OWN : 16 * (i // 2) + 16, (i % 2) * LANES : (i % 2 + 1) * LANES]
        bsend[i] = jnp.concatenate([conv, corr], axis=0).astype(BF16)

    def send_back(to):
        send(bsend.at[to], back.at[me], 2, (to, ten)).start()

    half_peers(send_back, 0)
    half_peers(send_grad, 1, cores=1)
    half_peers(send_back, 1)
    back[me] = bsend[me]

    some_grads = grads.at[pl.ds(0, half - 1)]
    send(some_grads, some_grads, 4, (me, ten)).wait_recv()
    square = jnp.sum(grads[:, 1:2, :], axis=0)
    tsend[...] = square
    for k in range(1, T):
        send(tsend, sizes.at[ten], 5, (me, lax.rem(ten + k, T))).start()
    sizes[ten] = square

    some_back = back.at[pl.ds(0, C - 1)]
    send(some_back, some_back, 2, (me, ten)).wait_recv()
    if T > 1:
        part = pl.ds(0, T - 1)
        send(sizes.at[part], sizes.at[part], 5, (me, ten)).wait_recv()

    send(some_taps, some_taps, 0, (me, ten)).wait_send()
    tap_swap.wait_send()
    send(msend.at[pl.ds(0, C - 1)], msend.at[pl.ds(0, C - 1)], 1, (me, ten)).wait_send()
    send(bsend.at[pl.ds(0, C - 1)], bsend.at[pl.ds(0, C - 1)], 2, (me, ten)).wait_send()
    swap.wait_send()

    send(some_grads, some_grads, 4, (me, ten)).wait_send()
    if T > 1:
        part = pl.ds(0, T - 1)
        send(sizes.at[part], sizes.at[part], 5, (me, ten)).wait_send()


def gates(
    C, entries,
    back, grads, sizes, q_ref, k_ref, v_ref, c_ref, scaled_product, scaled_gmix,
    mixed_hbm, gq_hbm, gk_hbm, gv_hbm, fg_hbm,
    mixed, gq, gk, gv, fg, store_sem,
):
    half = C // 2
    rows = C * OWN
    outs = [(mixed, mixed_hbm), (gq, gq_hbm), (gk, gk_hbm), (gv, gv_hbm), (fg, fg_hbm)]
    stores = [pltpu.make_async_copy(src, dst, store_sem.at[n]) for n, (src, dst) in enumerate(outs)]
    squared = jnp.sum(jnp.sum(sizes[...], axis=0), axis=1, keepdims=True)
    factor = jnp.minimum(1.0, math.sqrt(entries) / jnp.sqrt(squared + 1e-6))
    both = back[...].astype(F32)
    backward = both[:, OWN:].reshape(rows, LANES) + scaled_gmix[...]
    gk[...] = (backward * v_ref[...].astype(F32)).astype(BF16)
    stores[2].start()
    gv[...] = (backward * k_ref[...].astype(F32)).astype(BF16)
    stores[3].start()
    conv = jnp.dot(both[:, :OWN].reshape(rows, LANES).astype(BF16), exchange(), preferred_element_type=F32)
    forward = conv + scaled_product[...]
    mixed[...] = (q_ref[...].astype(F32) * forward).astype(BF16)
    stores[0].start()
    gq[...] = (c_ref[...].astype(F32) * forward).astype(BF16)
    stores[1].start()

    for r in range(half):
        fg[r : r + 1, :] = grads[r, 0:1, :] * factor
    stores[4].start()
    for store in stores:
        store.wait()


def per_device(C, T, query_slab, key_slab, value_slab, cotangent, filters, skip_gain):
    channels, tokens = query_slab.shape
    half = C // 2
    rows = C * OWN
    entries = half * T * tokens * C
    gains = skip_gain.reshape(channels // LANES, LANES)
    hbm_spec = pl.BlockSpec(memory_space=pltpu.HBM)
    slab = jax.ShapeDtypeStruct((channels, tokens), BF16)
    kept_slab = pltpu.VMEM((channels, tokens), BF16)
    kept_scaled = pltpu.VMEM((channels, tokens), F32)
    vmem_spec = pl.BlockSpec(memory_space=pltpu.VMEM)
    inputs = (query_slab, key_slab, value_slab, cotangent, filters, gains)
    kept = pl.pallas_call(
        functools.partial(kernel, C, T),
        out_shape=(
            pltpu.VMEM((C, 16, LANES), BF16),
            pltpu.VMEM((half, 2, LANES), F32),
            pltpu.VMEM((T, 1, LANES), F32),
            kept_slab, kept_slab, kept_slab, kept_slab, kept_scaled, kept_scaled,
        ),
        in_specs=[hbm_spec] * 6,
        out_specs=(vmem_spec,) * 9,
        scratch_shapes=[
            pltpu.VMEM((half, tokens), BF16),
            pltpu.VMEM(gains.shape, F32),
            pltpu.VMEM((half, 1, LANES), F32),
            pltpu.VMEM((2, half, 1, LANES), F32),
            pltpu.VMEM((C, 16, LANES), BF16),
            pltpu.VMEM((C, 16, LANES), BF16),
            pltpu.VMEM((C + 1, LANES, LANES), BF16),
            pltpu.VMEM((16 * (half + 4), 2 * LANES), BF16),
            pltpu.VMEM((16 * half, 2 * LANES), F32),
            pltpu.VMEM((2 * rows, 2 * LANES), BF16),
            pltpu.VMEM((C, 16, LANES), BF16),
            pltpu.VMEM((C, 1, LANES), F32),
            pltpu.VMEM((C, 1, LANES), F32),
            pltpu.VMEM((C, 2, LANES), F32),
            pltpu.VMEM((1, LANES), F32),
            pltpu.SemaphoreType.DMA((7,)),
            pltpu.SemaphoreType.DMA((7,)),
            pltpu.SemaphoreType.DMA((7,)),
        ],
        compiler_params=pltpu.CompilerParams(
            collective_id=0, has_side_effects=True, vmem_limit_bytes=VMEM_BYTES
        ),
        name="hyena",
    )(*(pltpu.with_memory_space_constraint(array, pltpu.HBM) for array in inputs))
    slab_buffer = pltpu.VMEM((channels, tokens), BF16)
    return pl.pallas_call(
        functools.partial(gates, C, entries),
        out_shape=(slab, slab, slab, slab, jax.ShapeDtypeStruct((half, tokens), F32)),
        in_specs=[vmem_spec] * 9,
        out_specs=(hbm_spec,) * 5,
        scratch_shapes=[
            slab_buffer, slab_buffer, slab_buffer, slab_buffer,
            pltpu.VMEM((half, tokens), F32),
            pltpu.SemaphoreType.DMA((5,)),
        ],
        compiler_params=pltpu.CompilerParams(vmem_limit_bytes=VMEM_BYTES),
        name="gates",
    )(*(pltpu.with_memory_space_constraint(array, pltpu.VMEM) for array in kept))


def solution(mesh):
    C, T = mesh.shape["context"], mesh.shape["tensor"]
    slab = P("tensor", "context")
    return jax.shard_map(
        functools.partial(per_device, C, T),
        mesh=mesh,
        in_specs=(slab, slab, slab, slab, slab, P("tensor")),
        out_specs=(slab, slab, slab, slab, slab),
        check_vma=False,
    )
```

```python
import functools
import math

import jax
import jax.numpy as jnp
from jax import lax
from jax.experimental import pallas as pl
from jax.experimental.pallas import tpu as pltpu
from jax.sharding import PartitionSpec as P

MESH = pl.DeviceIdType.MESH
F32 = jnp.float32
BF16 = jnp.bfloat16
LANES = 128
VMEM_BYTES = 32 * 1024 * 1024
SPLIT = 1
UNROLL = 16
OWN = 8


def exchange(lanes=LANES):
    row = lax.broadcasted_iota(jnp.int32, (lanes, lanes), 0)
    col = lax.broadcasted_iota(jnp.int32, (lanes, lanes), 1)
    return (row + col == lanes - 1).astype(BF16)


def far(i, n):
    return n // 2 + ((i + 1) // 2) * (1 - 2 * (i % 2))


def kernel(
    C, T,
    q_hbm, k_hbm, v_hbm, c_hbm, f_hbm, gain_hbm,
    back, grads, sizes, q_ref, k_ref, v_ref, c_ref, scaled_product, scaled_gmix,
    f_ref, gain_ref,
    fsend, frecv, msend, mrecv, toep, z2, acc, gcat, bsend,
    raw, raw_other, gsend, tsend,
    load_sem, send_sem, recv_sem,
):
    me = lax.axis_index("context")
    ten = lax.axis_index("tensor")
    half = C // 2
    Z, Y = 4, C // 8
    pair = me // 2
    z = pair // Y
    y = pair % Y
    core = me % 2
    rows = C * OWN

    def each_peer(start, cores=2, first=0, stop=Y):
        columns = []
        for j in range(Z):
            plane = lax.rem(z + far(j, Z), Z)
            columns += [2 * Y * plane + 1 - core, 2 * Y * plane + core][2 - cores :]
        ring(start, columns, False, first, stop)

    def ring(start, columns, last, first=0, stop=Y):
        def at(i, _):
            place = 2 * lax.rem(y + far(i, Y), Y)
            for column in columns:
                start(column + place)
            return 0

        lax.fori_loop(first, min(stop, Y - 1), at, 0)
        if stop < Y:
            return
        for column in columns[:-1]:
            start(column + 2 * y)
        if last is not False:
            pl.when(last)(lambda: start(columns[-1] + 2 * y))

    def half_peers(start, late, cores=2):
        for plane in (2 * late, 2 * late + 1):
            ring(start, [2 * Y * plane + 1 - core, 2 * Y * plane + core][2 - cores :], z != plane)

    def plane_peers(start, plane):
        ring(start, [2 * Y * plane + 1 - core, 2 * Y * plane + core], z != plane)

    barrier = pltpu.get_barrier_semaphore()
    each_peer(lambda to: pl.semaphore_signal(barrier, inc=1, device_id=(to, ten), device_id_type=MESH))
    for k in range(1, T):
        pl.semaphore_signal(barrier, inc=1, device_id=(me, lax.rem(ten + k, T)), device_id_type=MESH)

    loads = [
        pltpu.make_async_copy(src, dst, load_sem.at[n])
        for n, (src, dst) in enumerate(
            [(f_hbm, f_ref), (k_hbm, k_ref), (v_hbm, v_ref), (q_hbm, q_ref), (c_hbm, c_ref), (gain_hbm, gain_ref)]
        )
    ]
    for load in loads:
        load.start()

    flip = exchange()

    loads[0].wait()
    taps = jnp.dot(f_ref[...], flip, preferred_element_type=F32)
    for r in range(half):
        fsend[r] = taps[r : r + 1]

    for load in loads[1:5]:
        load.wait()
    product = (k_ref[...].astype(F32) * v_ref[...].astype(F32)).astype(BF16)
    mirrored = jnp.dot(product, flip, preferred_element_type=F32).reshape(C, OWN, LANES)
    gmix = (q_ref[...].astype(F32) * c_ref[...].astype(F32)).reshape(C, OWN, LANES)
    msend[...] = jnp.concatenate([mirrored, gmix], axis=1).astype(BF16)

    pl.semaphore_wait(barrier, C - 1 + T - 1)

    def send(src, dst, phase, peer):
        return pltpu.make_async_remote_copy(
            src_ref=src, dst_ref=dst, send_sem=send_sem.at[phase], recv_sem=recv_sem.at[phase],
            device_id=peer, device_id_type=MESH,
        )

    def send_main(to):
        send(msend.at[to], mrecv.at[me], 1, (to, ten)).start()

    def send_taps(to):
        send(fsend.at[to // 2], frecv.at[core, pair], 0, (to, ten)).start()

    each_peer(send_main, stop=SPLIT)
    each_peer(send_taps, cores=1)
    each_peer(send_main, first=SPLIT)

    frecv[core, pair] = fsend[pair]
    mrecv[me] = msend[me]
    loads[5].wait()
    for n in range(rows // LANES):
        lines = slice(n * LANES, (n + 1) * LANES)
        gain = jnp.broadcast_to(gain_ref[n : n + 1, :], (LANES, LANES)).T
        part = (k_ref[lines].astype(F32) * v_ref[lines].astype(F32)).astype(BF16)
        scaled_product[lines] = gain * part.astype(F32)
        part = (q_ref[lines].astype(F32) * c_ref[lines].astype(F32)).astype(BF16)
        scaled_gmix[lines] = gain * part.astype(F32)
    toep[0] = jnp.zeros((LANES, LANES), BF16)
    z2[half * 16 :, :] = jnp.zeros((z2.shape[0] - half * 16, 2 * LANES), BF16)
    gcat[rows:, :] = jnp.zeros((gcat.shape[0] - rows, 2 * LANES), BF16)

    row = lax.broadcasted_iota(jnp.int32, (LANES, LANES), 0)
    col = lax.broadcasted_iota(jnp.int32, (LANES, LANES), 1)
    lower = col <= row

    def skew(block):
        return pltpu.roll(block, 1, 1, stride=1, stride_axis=0)

    other = me + 1 - 2 * core
    some_taps = frecv.at[core, pl.ds(0, half - 1)]
    send(some_taps, some_taps, 0, (me, ten)).wait_recv()
    tap_swap = send(frecv.at[core], frecv.at[core], 6, (other, ten))
    tap_swap.start()

    send(mrecv.at[pl.ds(0, C - 1)], mrecv.at[pl.ds(0, C - 1)], 1, (me, ten)).wait_recv()
    zero = jnp.zeros((OWN, LANES), F32)
    whole = mrecv[...].astype(F32)
    xt = whole[:, :OWN].reshape(rows, LANES).T.astype(BF16)
    gpart = whole[:, OWN:]
    after = jnp.concatenate([gpart[1:], zero[None]], axis=0)
    gcat[0:rows, :] = jnp.concatenate([gpart, after], axis=2).reshape(rows, 2 * LANES).astype(BF16)

    def lags(e, depth):
        first = pl.multiple_of(16 * e, 16)
        return jnp.dot(xt[:, :depth], gcat[pl.ds(first, depth), :], preferred_element_type=F32)

    def gather(depth, group):
        def body(n, last):
            parts = [lags(group * n + u, depth) for u in range(group)]
            for u in reversed(range(group)):
                for side in (1, 0):
                    turned = skew(parts[u][:, side * LANES : (side + 1) * LANES])
                    place = 2 * (group * n + u) + side
                    raw[place] = jnp.sum(jnp.where(lower, turned, last), axis=0, keepdims=True)
                    last = turned
            return last

        return body

    group = min(8, half // 2)
    last = jnp.zeros((LANES, LANES), F32)
    for n in reversed(range(half // group)):
        depth = rows if 2 * group * n < half else rows // 2
        last = gather(depth, group)(n, last)

    swap = send(raw, raw_other, 3, (other, ten))
    swap.start()

    tap_swap.wait_recv()
    def build(n, last):
        for u in range(UNROLL):
            d = UNROLL * n + u
            turned = skew(jnp.broadcast_to(frecv[u % 2, d // 2], (LANES, LANES)))
            toep[d + 1] = jnp.where(lower, turned, last).astype(BF16)
            last = turned
        return last

    lax.fori_loop(0, C // UNROLL, build, jnp.zeros((LANES, LANES), F32))

    for j in range(half):
        two = []
        for i in (2 * j, 2 * j + 1):
            two.append(jnp.concatenate([mrecv[C - 1 - i].astype(F32)[:OWN], mrecv[i].astype(F32)[OWN:]], axis=0))
        z2[16 * j : 16 * j + 16, :] = jnp.concatenate(two, axis=1).astype(BF16)

    swap.wait_recv()
    total = raw[...] + raw_other[...]
    size = jnp.sum(total * total, axis=0)
    gsend[:, 0:1, :] = total
    gsend[:, 1:2, :] = jnp.broadcast_to(size[None], (C, 1, LANES))

    def send_grad(to):
        send(gsend.at[to], grads.at[pair], 4, (to, ten)).start()

    half_peers(send_grad, 0, cores=1)
    grads[pair] = gsend[me]

    def weight(d):
        top = jnp.concatenate([toep[2 * d + 1], toep[2 * d]], axis=1)
        low = jnp.concatenate([toep[2 * d + 2], toep[2 * d + 1]], axis=1)
        return jnp.concatenate([top, low], axis=0)

    step = min(4, half)
    for d0 in range(0, half, step):
        size = 16 * (half - d0)
        left = jnp.concatenate([z2[16 * (d0 + u) : 16 * (d0 + u) + size, :] for u in range(step)], axis=1)
        right = jnp.concatenate([weight(d0 + u) for u in range(step)], axis=0)
        part = jnp.dot(left, right, preferred_element_type=F32)
        if d0 == 0:
            acc[...] = part
        else:
            acc[0:size, :] += part

    for i in range(C):
        m = C - 1 - i
        conv = acc[16 * (m // 2) : 16 * (m // 2) + OWN, (m % 2) * LANES : (m % 2 + 1) * LANES]
        corr = acc[16 * (i // 2) + OWN : 16 * (i // 2) + 16, (i % 2) * LANES : (i % 2 + 1) * LANES]
        bsend[i] = jnp.concatenate([conv, corr], axis=0).astype(BF16)

    def send_back(to):
        send(bsend.at[to], back.at[me], 2, (to, ten)).start()

    half_peers(send_back, 0)
    half_peers(send_grad, 1, cores=1)
    back[me] = bsend[me]

    some_grads = grads.at[pl.ds(0, half - 1)]
    send(some_grads, some_grads, 4, (me, ten)).wait_recv()
    square = jnp.sum(grads[:, 1:2, :], axis=0)
    tsend[...] = square
    for k in range(1, T):
        send(tsend, sizes.at[ten], 5, (me, lax.rem(ten + k, T))).start()
    sizes[ten] = square
    half_peers(send_back, 1)

    some_back = back.at[pl.ds(0, C - 1)]
    send(some_back, some_back, 2, (me, ten)).wait_recv()
    if T > 1:
        part = pl.ds(0, T - 1)
        send(sizes.at[part], sizes.at[part], 5, (me, ten)).wait_recv()

    send(some_taps, some_taps, 0, (me, ten)).wait_send()
    tap_swap.wait_send()
    send(msend.at[pl.ds(0, C - 1)], msend.at[pl.ds(0, C - 1)], 1, (me, ten)).wait_send()
    send(bsend.at[pl.ds(0, C - 1)], bsend.at[pl.ds(0, C - 1)], 2, (me, ten)).wait_send()
    swap.wait_send()

    send(some_grads, some_grads, 4, (me, ten)).wait_send()
    if T > 1:
        part = pl.ds(0, T - 1)
        send(sizes.at[part], sizes.at[part], 5, (me, ten)).wait_send()


def gates(
    C, entries,
    back, grads, sizes, q_ref, k_ref, v_ref, c_ref, scaled_product, scaled_gmix,
    mixed_hbm, gq_hbm, gk_hbm, gv_hbm, fg_hbm,
    mixed, gq, gk, gv, fg, store_sem,
):
    half = C // 2
    rows = C * OWN
    outs = [(mixed, mixed_hbm), (gq, gq_hbm), (gk, gk_hbm), (gv, gv_hbm), (fg, fg_hbm)]
    stores = [pltpu.make_async_copy(src, dst, store_sem.at[n]) for n, (src, dst) in enumerate(outs)]
    squared = jnp.sum(jnp.sum(sizes[...], axis=0), axis=1, keepdims=True)
    factor = jnp.minimum(1.0, math.sqrt(entries) / jnp.sqrt(squared + 1e-6))
    both = back[...].astype(F32)
    backward = both[:, OWN:].reshape(rows, LANES) + scaled_gmix[...]
    gk[...] = (backward * v_ref[...].astype(F32)).astype(BF16)
    stores[2].start()
    gv[...] = (backward * k_ref[...].astype(F32)).astype(BF16)
    stores[3].start()
    conv = jnp.dot(both[:, :OWN].reshape(rows, LANES).astype(BF16), exchange(), preferred_element_type=F32)
    forward = conv + scaled_product[...]
    mixed[...] = (q_ref[...].astype(F32) * forward).astype(BF16)
    stores[0].start()
    gq[...] = (c_ref[...].astype(F32) * forward).astype(BF16)
    stores[1].start()

    for r in range(half):
        fg[r : r + 1, :] = grads[r, 0:1, :] * factor
    stores[4].start()
    for store in stores:
        store.wait()


def per_device(C, T, query_slab, key_slab, value_slab, cotangent, filters, skip_gain):
    channels, tokens = query_slab.shape
    half = C // 2
    rows = C * OWN
    entries = half * T * tokens * C
    gains = skip_gain.reshape(channels // LANES, LANES)
    hbm_spec = pl.BlockSpec(memory_space=pltpu.HBM)
    slab = jax.ShapeDtypeStruct((channels, tokens), BF16)
    kept_slab = pltpu.VMEM((channels, tokens), BF16)
    kept_scaled = pltpu.VMEM((channels, tokens), F32)
    vmem_spec = pl.BlockSpec(memory_space=pltpu.VMEM)
    inputs = (query_slab, key_slab, value_slab, cotangent, filters, gains)
    kept = pl.pallas_call(
        functools.partial(kernel, C, T),
        out_shape=(
            pltpu.VMEM((C, 16, LANES), BF16),
            pltpu.VMEM((half, 2, LANES), F32),
            pltpu.VMEM((T, 1, LANES), F32),
            kept_slab, kept_slab, kept_slab, kept_slab, kept_scaled, kept_scaled,
        ),
        in_specs=[hbm_spec] * 6,
        out_specs=(vmem_spec,) * 9,
        scratch_shapes=[
            pltpu.VMEM((half, tokens), BF16),
            pltpu.VMEM(gains.shape, F32),
            pltpu.VMEM((half, 1, LANES), F32),
            pltpu.VMEM((2, half, 1, LANES), F32),
            pltpu.VMEM((C, 16, LANES), BF16),
            pltpu.VMEM((C, 16, LANES), BF16),
            pltpu.VMEM((C + 1, LANES, LANES), BF16),
            pltpu.VMEM((16 * (half + 4), 2 * LANES), BF16),
            pltpu.VMEM((16 * half, 2 * LANES), F32),
            pltpu.VMEM((2 * rows, 2 * LANES), BF16),
            pltpu.VMEM((C, 16, LANES), BF16),
            pltpu.VMEM((C, 1, LANES), F32),
            pltpu.VMEM((C, 1, LANES), F32),
            pltpu.VMEM((C, 2, LANES), F32),
            pltpu.VMEM((1, LANES), F32),
            pltpu.SemaphoreType.DMA((7,)),
            pltpu.SemaphoreType.DMA((7,)),
            pltpu.SemaphoreType.DMA((7,)),
        ],
        compiler_params=pltpu.CompilerParams(
            collective_id=0, has_side_effects=True, vmem_limit_bytes=VMEM_BYTES
        ),
        name="hyena",
    )(*(pltpu.with_memory_space_constraint(array, pltpu.HBM) for array in inputs))
    slab_buffer = pltpu.VMEM((channels, tokens), BF16)
    return pl.pallas_call(
        functools.partial(gates, C, entries),
        out_shape=(slab, slab, slab, slab, jax.ShapeDtypeStruct((half, tokens), F32)),
        in_specs=[vmem_spec] * 9,
        out_specs=(hbm_spec,) * 5,
        scratch_shapes=[
            slab_buffer, slab_buffer, slab_buffer, slab_buffer,
            pltpu.VMEM((half, tokens), F32),
            pltpu.SemaphoreType.DMA((5,)),
        ],
        compiler_params=pltpu.CompilerParams(vmem_limit_bytes=VMEM_BYTES),
        name="gates",
    )(*(pltpu.with_memory_space_constraint(array, pltpu.VMEM) for array in kept))


def solution(mesh):
    C, T = mesh.shape["context"], mesh.shape["tensor"]
    slab = P("tensor", "context")
    return jax.shard_map(
        functools.partial(per_device, C, T),
        mesh=mesh,
        in_specs=(slab, slab, slab, slab, slab, P("tensor")),
        out_specs=(slab, slab, slab, slab, slab),
        check_vma=False,
    )
```
